256 devices in a mesh: seq: 64 (over y, z, core), grp: 4 (over x).
Axes of the slice: x: 4, y: 4, z: 8, core: 2. Of those that a mesh axis runs over, the one named last changes fastest.
Arguments:
- queries: bfloat16 [32768, 2048], P(('grp', 'seq')), may hold values from -6 to 6
- key_row_matrix: bfloat16 [32768, 2048], P(('grp', 'seq')), may hold values from -6 to 6
- value_row_matrix: bfloat16 [32768, 2048], P(('grp', 'seq')), may hold values from -6 to 6
- output_gradient: bfloat16 [32768, 2048], P(('grp', 'seq')), may hold values from -6 to 6
Outputs:
- query_gradient: bfloat16 [32768, 2048], P(('grp', 'seq'))
- key_gradient: bfloat16 [32768, 2048], P(('grp', 'seq'))
- value_gradient: bfloat16 [32768, 2048], P(('grp', 'seq'))
The draws below stay inside these ranges and needn't reach their ends.
All inputs are finite; a program needn't handle non-finite values.
Results may differ from the reference program's by a relative error of at most 0.005.
Values sent between devices are 32-bit elements; how exact they have to be, the bound alone decides.
No kernel may reach another device: no remote copies, remote signals or barrier semaphores. Data moves between devices by JAX's collectives and lax.ppermute only.
A program may use at most 320 MiB of HBM per device.

```python
import jax
import jax.numpy as jnp
from jax import lax

HEADS = 16
HEAD = 128
TOK_DEV = 128
TOKENS = 32768


def steps_of(key, shape, cuts, smallest, top_value):
    def one(dim, blocks):
        draws = jax.random.uniform(jax.random.fold_in(jax.random.fold_in(key, 6), dim), (blocks,), jnp.float32, smallest / len(cuts), top_value / len(cuts))
        return jnp.repeat(jnp.exp(draws), shape[dim] // blocks).reshape((-1,) + (1,) * (len(shape) - dim - 1))

    gain = one(*cuts[0])
    for cut in cuts[1:]:
        gain = gain * one(*cut)
    return gain


def gaussian(stream_key, dims, deviation, most, shards=(), kind=jnp.bfloat16):
    result = jax.random.normal(stream_key, dims, jnp.float32) * deviation
    if len(shards) > 0:
        result = steps_of(stream_key, dims, shards, -0.22, 0.18) * result
    return jnp.clip(result, min=-most, max=most).astype(kind)


def setup_inputs(seed: int = 0) -> dict:
    key_list = jax.random.split(jax.random.key(seed), 5)
    return {
        "queries": gaussian(key_list[0], (TOKENS, HEADS * HEAD), 1.0, 6.0, ((0, 256),)),
        "key_row_matrix": gaussian(key_list[1], (TOKENS, HEADS * HEAD), 1.0, 6.0, ((0, 256),)),
        "value_row_matrix": gaussian(key_list[2], (TOKENS, HEADS * HEAD), 1.0, 6.0, ((0, 256),)),
        "output_gradient": gaussian(key_list[3], (TOKENS, HEADS * HEAD), 1.0, 6.0, ((0, 256),)),
    }


def block_grads(queries, key_row_matrix, value_row_matrix, output_gradient, prefix_key_value, suffix_query_output, scale_factor):
    count = queries.shape[0]
    position = jnp.arange(count)
    causal = position[:, None] >= position[None, :]
    query_flat = queries.astype(jnp.float32)
    key_flat = key_row_matrix.astype(jnp.float32)
    value_flat = value_row_matrix.astype(jnp.float32)
    gradient_flat = output_gradient.astype(jnp.float32)
    score_dv = jnp.einsum("thd,shd->hts", gradient_flat, value_flat)
    score_qk = jnp.einsum("thd,shd->hts", query_flat, key_flat)
    weight_value_gradient = jnp.where(causal[None], scale_factor * score_dv, 0.0).astype(jnp.bfloat16).astype(jnp.float32)
    weight_query_key = jnp.where(causal[None], scale_factor * score_qk, 0.0).astype(jnp.bfloat16).astype(jnp.float32)
    prefix_flat = prefix_key_value.astype(jnp.float32)
    suffix_flat = suffix_query_output.astype(jnp.float32)
    query_gradient = scale_factor * jnp.einsum("rsp,sap->rsa", gradient_flat, prefix_flat) + jnp.einsum("eop,pez->oez", weight_value_gradient, key_flat)
    key_gradient = scale_factor * jnp.einsum("mjr,jdr->mjd", value_flat, suffix_flat) + jnp.einsum("rlz,lrq->zrq", weight_value_gradient, query_flat)
    value_gradient = scale_factor * jnp.einsum("nba,bal->nbl", key_flat, suffix_flat) + jnp.einsum("fbd,bfq->dfq", weight_query_key, gradient_flat)
    return query_gradient.astype(jnp.bfloat16), key_gradient.astype(jnp.bfloat16), value_gradient.astype(jnp.bfloat16)


def block_states(pieces):
    queries, key_row_matrix, value_row_matrix, output_gradient = pieces
    key_value_state = jnp.einsum("cqe,cqg->qeg", key_row_matrix.astype(jnp.float32), value_row_matrix.astype(jnp.float32))
    query_output_state = jnp.einsum("jmb,jmf->mbf", queries.astype(jnp.float32), output_gradient.astype(jnp.float32))
    return key_value_state, query_output_state


def reference(queries, key_row_matrix, value_row_matrix, output_gradient):
    blocks = TOKENS // TOK_DEV
    shaped = (blocks, TOK_DEV, HEADS, HEAD)
    query_b = queries.reshape(shaped)
    key_b = key_row_matrix.reshape(shaped)
    value_b = value_row_matrix.reshape(shaped)
    grad_b = output_gradient.reshape(shaped)
    key_value_state, query_output_state = lax.map(block_states, (query_b, key_b, value_b, grad_b))
    empty = jnp.zeros_like(key_value_state[:1])
    prefix_key_value = jnp.concatenate([empty, jnp.cumsum(key_value_state, axis=0)[:-1]], axis=0).astype(jnp.bfloat16)
    later = jnp.cumsum(query_output_state[::-1], axis=0)[::-1]
    suffix_query_output = jnp.concatenate([later[1:], empty], axis=0).astype(jnp.bfloat16)
    scale_factor = float(HEAD * TOKENS) ** -0.5

    def one_block(pieces):
        return block_grads(pieces[0], pieces[1], pieces[2], pieces[3], pieces[4], pieces[5], scale_factor)

    query_gradient, key_gradient, value_gradient = lax.map(one_block, (query_b, key_b, value_b, grad_b, prefix_key_value, suffix_query_output))
    flat = (TOKENS, HEADS * HEAD)
    return query_gradient.reshape(flat), key_gradient.reshape(flat), value_gradient.reshape(flat)
```

```python
import functools

import jax
import jax.numpy as jnp
from jax import lax
from jax.experimental import pallas as pl
from jax.experimental.pallas import tpu as pltpu
from jax.sharding import Mesh
from jax.sharding import PartitionSpec as P

HEAD = 128
HEADS_PER_STEP = 4
CHIP_AXES = ("x", "y", "z")
ROWS = ("x", "y", "z", "c")
FLAG = pl.BlockSpec(memory_space=pltpu.SMEM)
VMEM_LIMIT = 24 * 1024 * 1024


def tokens_spec(count):
    return pl.BlockSpec((count, HEADS_PER_STEP * HEAD), lambda i: (0, i))


def states_spec():
    return pl.BlockSpec((HEADS_PER_STEP * HEAD, HEAD), lambda i: (i, 0))


def contract(lhs, rhs, lhs_dim, rhs_dim):
    return lax.dot_general(
        lhs, rhs, (((lhs_dim,), (rhs_dim,)), ((), ())), preferred_element_type=jnp.float32
    )


def states_kernel(core, query, key, value, gradient, keep, send):
    first = core[0] == 0
    for h in range(HEADS_PER_STEP):
        lanes = pl.ds(h * HEAD, HEAD)
        kv = contract(key[:, lanes], value[:, lanes], 0, 0)
        qo = contract(query[:, lanes], gradient[:, lanes], 0, 0)
        keep[lanes, :] = jnp.where(first, kv, qo)
        send[lanes, :] = jnp.where(first, qo, kv)


def weights_kernel(query, key, value, gradient, weight_dv, weight_qk):
    count = query.shape[0]
    causal = lax.broadcasted_iota(jnp.int32, (count, count), 0) >= lax.broadcasted_iota(
        jnp.int32, (count, count), 1
    )
    for h in range(HEADS_PER_STEP):
        lanes = pl.ds(h * HEAD, HEAD)
        dv = contract(gradient[:, lanes], value[:, lanes], 1, 1)
        qk = contract(query[:, lanes], key[:, lanes], 1, 1)
        weight_dv[:, lanes] = jnp.where(causal, dv, 0.0).astype(jnp.bfloat16)
        weight_qk[:, lanes] = jnp.where(causal, qk, 0.0).astype(jnp.bfloat16)


def scan_kernel(core, parts, out):
    count = parts.shape[0]
    reverse = core[0] == 1

    def step(i, total):
        place = jnp.where(reverse, count - 1 - i, i)
        out[place] = total
        return total + parts[place]

    lax.fori_loop(0, count, step, jnp.zeros(parts.shape[1:], jnp.float32), unroll=8)


def outputs_kernel(
    scale, core, query, key, value, gradient, weight_dv, weight_qk, own, recv, other, gq, gk, gv
):
    first = core[0] == 0
    for h in range(HEADS_PER_STEP):
        lanes = pl.ds(h * HEAD, HEAD)
        mine = own[lanes, :]
        theirs = recv[lanes, :] + other[lanes, :]
        prefix = jnp.where(first, mine, theirs).astype(jnp.bfloat16)
        suffix = jnp.where(first, theirs, mine).astype(jnp.bfloat16)
        q, k, v, g = query[:, lanes], key[:, lanes], value[:, lanes], gradient[:, lanes]
        dv, qk = weight_dv[:, lanes], weight_qk[:, lanes]
        gq[:, lanes] = (scale * (contract(g, prefix, 1, 1) + contract(dv, k, 1, 0))).astype(
            jnp.bfloat16
        )
        gk[:, lanes] = (scale * (contract(v, suffix, 1, 1) + contract(dv, q, 0, 0))).astype(
            jnp.bfloat16
        )
        gv[:, lanes] = (scale * (contract(k, suffix, 1, 0) + contract(qk, g, 0, 0))).astype(
            jnp.bfloat16
        )


def call(kernel, in_specs, out_specs, out_shape, grid, flops, moved):
    return pl.pallas_call(
        kernel,
        in_specs=in_specs,
        out_specs=out_specs,
        out_shape=out_shape,
        grid=grid,
        cost_estimate=pl.CostEstimate(flops=flops, bytes_accessed=moved, transcendentals=0),
        compiler_params=pltpu.CompilerParams(vmem_limit_bytes=VMEM_LIMIT),
    )


def per_device(chips, scale, queries, key_row_matrix, value_row_matrix, output_gradient):
    tokens, width = queries.shape
    heads = width // HEAD
    grid = (heads // HEADS_PER_STEP,)
    core = lax.axis_index("c").astype(jnp.int32).reshape(1)
    swap = [(0, 1), (1, 0)]
    product = 2 * heads * tokens * HEAD * HEAD
    token_bytes = 2 * tokens * width
    state_shape = jax.ShapeDtypeStruct((width, HEAD), jnp.float32)
    token_shape = jax.ShapeDtypeStruct((tokens, width), jnp.bfloat16)
    inputs = (queries, key_row_matrix, value_row_matrix, output_gradient)
    token = tokens_spec(tokens)
    state = states_spec()

    keep, send = call(
        states_kernel,
        [FLAG] + [token] * 4,
        [state] * 2,
        [state_shape] * 2,
        grid,
        2 * product,
        4 * token_bytes + 8 * width * HEAD,
    )(core, *inputs)
    recv = lax.ppermute(send, "c", swap)
    weight_dv, weight_qk = call(
        weights_kernel,
        [token] * 4,
        [token] * 2,
        [token_shape] * 2,
        grid,
        2 * product,
        6 * token_bytes,
    )(*inputs)
    other = lax.ppermute(keep, "c", swap)
    chip_state = (keep + recv).reshape(chips, width // chips, HEAD)
    parts = lax.all_to_all(chip_state, CHIP_AXES, 0, 0, tiled=True)
    scanned = call(
        scan_kernel,
        [FLAG, pl.BlockSpec(memory_space=pltpu.VMEM)],
        pl.BlockSpec(memory_space=pltpu.VMEM),
        jax.ShapeDtypeStruct(parts.shape, jnp.float32),
        (),
        width * HEAD,
        8 * width * HEAD,
    )(core, parts)
    own = lax.all_to_all(scanned, CHIP_AXES, 0, 0, tiled=True).reshape(width, HEAD)
    theirs = lax.ppermute(own, "c", swap)
    return call(
        functools.partial(outputs_kernel, scale),
        [FLAG] + [token] * 6 + [state] * 3,
        [token] * 3,
        [token_shape] * 3,
        grid,
        6 * product,
        9 * token_bytes + 12 * width * HEAD,
    )(core, *inputs, weight_dv, weight_qk, own, theirs, other)


def solution(mesh):
    fine = Mesh(mesh.devices.reshape(4, 8, 2, 4), ("y", "z", "c", "x"))
    chips = mesh.devices.size // 2

    def program(queries, key_row_matrix, value_row_matrix, output_gradient):
        scale = float(HEAD * queries.shape[0]) ** -0.5
        spec = P(ROWS, None)
        return jax.shard_map(
            functools.partial(per_device, chips, scale),
            mesh=fine,
            in_specs=(spec,) * 4,
            out_specs=(spec,) * 3,
            check_vma=False,
        )(queries, key_row_matrix, value_row_matrix, output_gradient)

    return program
```

```python
import functools

import jax
import jax.numpy as jnp
from jax import lax
from jax.experimental import pallas as pl
from jax.experimental.pallas import tpu as pltpu
from jax.sharding import Mesh
from jax.sharding import PartitionSpec as P

HEAD = 128
ROWS = ("x", "y", "z", "c")
SMEM = pl.BlockSpec(memory_space=pltpu.SMEM)
VMEM = pl.BlockSpec(memory_space=pltpu.VMEM)
HBM = pl.BlockSpec(memory_space=pltpu.HBM)
VMEM_LIMIT = 24 * 1024 * 1024
F32, BF16 = jnp.float32, jnp.bfloat16


def contract(lhs, rhs, lhs_dim, rhs_dim):
    return lax.dot_general(
        lhs, rhs, (((lhs_dim,), (rhs_dim,)), ((), ())), preferred_element_type=F32
    )


def chunk_lanes(index, width):
    return pl.ds(pl.multiple_of(index * width, width), width)


def states_kernel(places, query, key, value, gradient, keep, send, held, sems):
    first = places[0] == 0
    z = places[1]
    slots = keep.shape[0]
    width = keep.shape[1]
    copies = []
    for slot in range(slots):
        lanes = chunk_lanes(lax.rem(z + slot, slots), width)
        for n, source in enumerate((key, value, query, gradient)):
            copy = pltpu.make_async_copy(
                source.at[:, lanes], held.at[n, slot], sems.at[n, slot]
            )
            copy.start()
            copies.append(copy)
    for slot in range(slots):
        for copy in copies[4 * slot : 4 * slot + 4]:
            copy.wait()
        for h in range(width // HEAD):
            lanes = pl.ds(h * HEAD, HEAD)
            kv = contract(held[0, slot, :, lanes], held[1, slot, :, lanes], 0, 0)
            qo = contract(held[2, slot, :, lanes], held[3, slot, :, lanes], 0, 0)
            keep[slot, lanes, :] = jnp.where(first, kv, qo)
            send[slot, lanes, :] = jnp.where(first, qo, kv)


def weights_kernel(query, key, value, gradient, dv, dv_turned, qk_turned):
    count = query.shape[0]
    row = lax.broadcasted_iota(jnp.int32, (count, count), 0)
    column = lax.broadcasted_iota(jnp.int32, (count, count), 1)
    for h in range(query.shape[1] // HEAD):
        lanes = pl.ds(h * HEAD, HEAD)
        q, k, v, g = query[:, lanes], key[:, lanes], value[:, lanes], gradient[:, lanes]
        dv[:, lanes] = jnp.where(row >= column, contract(g, v, 1, 1), 0.0).astype(BF16)
        dv_turned[:, lanes] = jnp.where(row <= column, contract(v, g, 1, 1), 0.0).astype(BF16)
        qk_turned[:, lanes] = jnp.where(row <= column, contract(k, q, 1, 1), 0.0).astype(BF16)


def merge_kernel(keep, received, *outs):
    for slot, out in enumerate(outs):
        out[...] = keep[slot] + received[slot]


def scan_kernel(slots, places, *refs):
    sources, extras, outs, held = (
        refs[:slots],
        refs[slots:-slots - 1],
        refs[-slots - 1 : -1],
        refs[-1],
    )
    reverse = places[0] == 1
    z = places[1]
    for k in range(slots):
        held[lax.rem(z + slots - k, slots)] = sources[k][...]
    total = extras[0][...]
    for extra in extras[1:]:
        total = total + extra[...]
    for n in range(slots):
        place = jnp.where(reverse, slots - 1 - n, n)
        piece = held[place]
        held[place] = total
        total = total + piece
    for k in range(slots):
        outs[k][...] = held[lax.rem(z + k, slots)]


def outputs_kernel(slots, scale, places, *refs):
    query, key, value, gradient, dv, dv_turned, qk_turned, other = refs[:8]
    own = refs[8 : 8 + slots]
    received = refs[8 + slots : 8 + 2 * slots]
    outs = refs[8 + 2 * slots : 11 + 2 * slots]
    held, sems = refs[11 + 2 * slots :]
    first = places[0] == 0
    z = places[1]
    width = own[0].shape[0]
    copies = []
    for k in range(slots):
        chunk = lax.rem(z + slots - k, slots)
        for h in range(width // HEAD):
            rows = pl.ds(h * HEAD, HEAD)
            mine = own[k][rows, :]
            theirs = received[k][rows, :] + other[(slots - k) % slots, rows, :]
            prefix = jnp.where(first, mine, theirs).astype(BF16)
            suffix = jnp.where(first, theirs, mine).astype(BF16)
            lanes = chunk_lanes(chunk * (width // HEAD) + h, HEAD)
            q, kk, v, g = query[:, lanes], key[:, lanes], value[:, lanes], gradient[:, lanes]
            gq = contract(g, prefix, 1, 1) + contract(dv[:, lanes], kk, 1, 0)
            gk = contract(v, suffix, 1, 1) + contract(dv_turned[:, lanes], q, 1, 0)
            gv = contract(kk, suffix, 1, 0) + contract(qk_turned[:, lanes], g, 1, 0)
            for n, result in enumerate((gq, gk, gv)):
                held[n, k, :, rows] = (scale * result).astype(BF16)
        for n, out in enumerate(outs):
            copy = pltpu.make_async_copy(
                held.at[n, k], out.at[:, chunk_lanes(chunk, width)], sems.at[n, k]
            )
            copy.start()
            copies.append(copy)
    for copy in copies:
        copy.wait()


def call(kernel, in_specs, out_specs, out_shape, flops, moved, scratch=()):
    return pl.pallas_call(
        kernel,
        in_specs=in_specs,
        out_specs=out_specs,
        out_shape=out_shape,
        scratch_shapes=scratch,
        cost_estimate=pl.CostEstimate(flops=flops, bytes_accessed=moved, transcendentals=0),
        compiler_params=pltpu.CompilerParams(vmem_limit_bytes=VMEM_LIMIT),
    )


def turn(array, axis, count, step):
    return lax.ppermute(array, axis, [(i, (i + step) % count) for i in range(count)])


def onward(array, axis, count, step):
    pairs = [(i, i + step) for i in range(count - step)]
    pairs += [(count + i, count + i - step) for i in range(step, count)]
    return lax.ppermute(array, ("c", axis), pairs)


def issue_order(count):
    return sorted(range(1, count), key=lambda k: (-(2 * k == count), min(k, count - k)))


def per_device(sizes, scale, queries, key_row_matrix, value_row_matrix, output_gradient):
    tokens, width = queries.shape
    slots = sizes["z"]
    chunk = width // slots
    core = lax.axis_index("c").astype(jnp.int32)
    depth = lax.axis_index("z").astype(jnp.int32)
    row = lax.axis_index("y").astype(jnp.int32)
    places = jnp.stack([core, depth])
    swap = [(0, 1), (1, 0)]
    product = 2 * width * tokens * HEAD
    token_bytes = 2 * tokens * width
    state_bytes = 4 * width * HEAD
    token_shape = jax.ShapeDtypeStruct((tokens, width), BF16)
    state_shape = jax.ShapeDtypeStruct((slots, chunk, HEAD), F32)
    chunk_shape = jax.ShapeDtypeStruct((chunk, HEAD), F32)
    inputs = (queries, key_row_matrix, value_row_matrix, output_gradient)

    keep, send = call(
        states_kernel,
        [SMEM] + [HBM] * 4,
        [VMEM] * 2,
        [state_shape] * 2,
        2 * product,
        4 * token_bytes + 2 * state_bytes,
        [
            pltpu.VMEM((4, slots, tokens, chunk), BF16),
            pltpu.SemaphoreType.DMA((4, slots)),
        ],
    )(places, *(pltpu.with_memory_space_constraint(a, pltpu.HBM) for a in inputs))
    received = lax.ppermute(send, "c", swap)
    weights = call(
        weights_kernel,
        [VMEM] * 4,
        [VMEM] * 3,
        [token_shape] * 3,
        3 * product,
        7 * token_bytes,
    )(*inputs)
    pieces = call(
        merge_kernel,
        [VMEM] * 2,
        [VMEM] * slots,
        [chunk_shape] * slots,
        width * HEAD,
        3 * state_bytes,
    )(keep, received)
    other = lax.ppermute(keep, "c", swap)

    gathered = list(pieces)
    for k in issue_order(slots):
        gathered[k] = turn(pieces[k], "z", slots, k)
    gathered, weights = lax.optimization_barrier((gathered, weights))
    column = functools.reduce(jnp.add, gathered)
    rows = sizes["y"]
    around = [turn(column, "y", rows, k) for k in range(1, rows)]
    plane = functools.reduce(jnp.add, around, column)
    before = functools.reduce(
        jnp.add,
        [
            jnp.where((row >= k) == (core == 0), part, 0.0)
            for k, part in enumerate(around, 1)
        ],
    )
    planes = [onward(plane, "x", sizes["x"], k) for k in range(1, sizes["x"])]
    prefixes = call(
        functools.partial(scan_kernel, slots),
        [SMEM] + [VMEM] * (slots + 1 + len(planes)),
        [VMEM] * slots,
        [chunk_shape] * slots,
        2 * width * HEAD,
        3 * state_bytes,
        [pltpu.VMEM((slots, chunk, HEAD), F32)],
    )(places, *gathered, before, *planes)
    own = list(prefixes)
    for k in issue_order(slots):
        own[k] = turn(prefixes[k], "z", slots, k)
    theirs = [lax.ppermute(part, "c", swap) for part in own]
    return call(
        functools.partial(outputs_kernel, slots, scale),
        [SMEM] + [VMEM] * (8 + 2 * slots),
        [HBM] * 3,
        [token_shape] * 3,
        6 * product,
        10 * token_bytes + 3 * state_bytes,
        [
            pltpu.VMEM((3, slots, tokens, chunk), BF16),
            pltpu.SemaphoreType.DMA((3, slots)),
        ],
    )(places, *inputs, *weights, other, *own, *theirs)


def solution(mesh):
    sizes = {"y": 4, "z": 8, "c": 2, "x": 4}
    fine = Mesh(mesh.devices.reshape(tuple(sizes.values())), tuple(sizes))

    def program(queries, key_row_matrix, value_row_matrix, output_gradient):
        scale = float(HEAD * queries.shape[0]) ** -0.5
        spec = P(ROWS, None)
        return jax.shard_map(
            functools.partial(per_device, sizes, scale),
            mesh=fine,
            in_specs=(spec,) * 4,
            out_specs=(spec,) * 3,
            check_vma=False,
        )(queries, key_row_matrix, value_row_matrix, output_gradient)

    return program
```

```python
import functools

import jax
import jax.numpy as jnp
from jax import lax
from jax.experimental import pallas as pl
from jax.experimental.pallas import tpu as pltpu
from jax.sharding import Mesh
from jax.sharding import PartitionSpec as P

HEAD = 128
LOADS = 4
ROWS = ("x", "y", "z", "c")
SMEM = pl.BlockSpec(memory_space=pltpu.SMEM)
VMEM = pl.BlockSpec(memory_space=pltpu.VMEM)
HBM = pl.BlockSpec(memory_space=pltpu.HBM)
VMEM_LIMIT = 24 * 1024 * 1024
F32, BF16 = jnp.float32, jnp.bfloat16


def contract(lhs, rhs, lhs_dim, rhs_dim):
    return lax.dot_general(
        lhs, rhs, (((lhs_dim,), (rhs_dim,)), ((), ())), preferred_element_type=F32
    )


def chunk_lanes(index, width):
    return pl.ds(pl.multiple_of(index * width, width), width)


def states_kernel(places, query, key, value, gradient, keep, send, held, sems):
    first = places[0] == 0
    z = places[1]
    slots = keep.shape[0]
    width = keep.shape[1]
    part = held.shape[3]
    copies = []
    for n in range(held.shape[1]):
        for source, tensor in enumerate((key, value, query, gradient)):
            copy = pltpu.make_async_copy(
                tensor.at[:, pl.ds(n * part, part)], held.at[source, n], sems.at[source, n]
            )
            copy.start()
            copies.append(copy)
    for n in range(held.shape[1]):
        for copy in copies[4 * n : 4 * n + 4]:
            copy.wait()
        for h in range(part // HEAD):
            lanes = pl.ds(h * HEAD, HEAD)
            chunk, row = divmod(n * part + h * HEAD, width)
            slot = lax.rem(chunk + slots - z, slots)
            kv = contract(held[0, n, :, lanes], held[1, n, :, lanes], 0, 0)
            qo = contract(held[2, n, :, lanes], held[3, n, :, lanes], 0, 0)
            keep[slot, pl.ds(row, HEAD), :] = jnp.where(first, kv, qo)
            send[slot, pl.ds(row, HEAD), :] = jnp.where(first, qo, kv)


def inner_kernel(query, key, value, gradient, gq, gk, gv):
    count = query.shape[0]
    causal = lax.broadcasted_iota(jnp.int32, (count, count), 0) >= lax.broadcasted_iota(
        jnp.int32, (count, count), 1
    )
    for h in range(query.shape[1] // HEAD):
        lanes = pl.ds(h * HEAD, HEAD)
        q, k, v, g = query[:, lanes], key[:, lanes], value[:, lanes], gradient[:, lanes]
        dv = jnp.where(causal, contract(g, v, 1, 1), 0.0).astype(BF16)
        qk = jnp.where(causal, contract(q, k, 1, 1), 0.0).astype(BF16)
        gq[:, lanes] = contract(dv, k, 1, 0)
        gk[:, lanes] = contract(dv, q, 0, 0)
        gv[:, lanes] = contract(qk, g, 0, 0)


def merge_kernel(order, keep, received, *outs):
    for offset, out in zip(order, outs, strict=True):
        out[...] = keep[offset] + received[offset]


def sum_kernel(*refs):
    total = refs[0][...]
    for ref in refs[1:-1]:
        total = total + ref[...]
    refs[-1][...] = total


def scan_kernel(order, rows, places, *refs):
    slots = len(order)
    sources = refs[:slots]
    around = refs[slots : slots + rows - 1]
    planes = refs[slots + rows - 1 : -slots - 1]
    outs = refs[-slots - 1 : -1]
    held = refs[-1]
    first = places[0] == 0
    z = places[1]
    row = places[2]
    total = planes[0][...]
    for plane in planes[1:]:
        total = total + plane[...]
    for step, part in enumerate(around, 1):
        total = total + jnp.where((row >= step) == first, part[...], 0.0)
    for offset, source in zip(order, sources, strict=True):
        held[lax.rem(z + slots - offset, slots)] = source[...]
    for n in range(slots):
        place = jnp.where(first, n, slots - 1 - n)
        piece = held[place]
        held[place] = total
        total = total + piece
    for offset, out in zip(order, outs, strict=True):
        out[...] = held[lax.rem(z + offset, slots)]


def outputs_kernel(order, scale, places, *refs):
    slots = len(order)
    query, key, value, gradient = refs[:4]
    inner = refs[4:7]
    other = refs[7]
    own = refs[8 : 8 + slots]
    received = refs[8 + slots : 8 + 2 * slots]
    outs = refs[8 + 2 * slots : 11 + 2 * slots]
    held, sems = refs[11 + 2 * slots :]
    first = places[0] == 0
    z = places[1]
    width = own[0].shape[0]
    copies = []
    for n, offset in enumerate(order):
        chunk = lax.rem(z + slots - offset, slots)
        for h in range(width // HEAD):
            rows = pl.ds(h * HEAD, HEAD)
            mine = own[n][rows, :]
            theirs = received[n][rows, :] + other[(slots - offset) % slots, rows, :]
            prefix = jnp.where(first, mine, theirs).astype(BF16)
            suffix = jnp.where(first, theirs, mine).astype(BF16)
            lanes = chunk_lanes(chunk * (width // HEAD) + h, HEAD)
            gq = contract(gradient[:, lanes], prefix, 1, 1)
            gk = contract(value[:, lanes], suffix, 1, 1)
            gv = contract(key[:, lanes], suffix, 1, 0)
            for t, result in enumerate((gq, gk, gv)):
                held[t, n, :, rows] = (scale * (result + inner[t][:, lanes])).astype(BF16)
        for t, out in enumerate(outs):
            copy = pltpu.make_async_copy(
                held.at[t, n], out.at[:, chunk_lanes(chunk, width)], sems.at[t, n]
            )
            copy.start()
            copies.append(copy)
    for copy in copies:
        copy.wait()


def call(kernel, in_specs, out_specs, out_shape, flops, moved, scratch=()):
    return pl.pallas_call(
        kernel,
        in_specs=in_specs,
        out_specs=out_specs,
        out_shape=out_shape,
        scratch_shapes=scratch,
        cost_estimate=pl.CostEstimate(flops=flops, bytes_accessed=moved, transcendentals=0),
        compiler_params=pltpu.CompilerParams(vmem_limit_bytes=VMEM_LIMIT),
    )


def turn(array, axis, count, step):
    return lax.ppermute(array, axis, [(i, (i + step) % count) for i in range(count)])


def onward(array, axis, count, step):
    pairs = [(i, i + step) for i in range(count - step)]
    pairs += [(count + i, count + i - step) for i in range(step, count)]
    return lax.ppermute(array, ("c", axis), pairs)


def issue_order(count):
    return sorted(range(count), key=lambda k: (k > 0, 2 * k != count, min(k, count - k), k))


def per_device(sizes, scale, queries, key_row_matrix, value_row_matrix, output_gradient):
    tokens, width = queries.shape
    slots = sizes["z"]
    rows = sizes["y"]
    order = issue_order(slots)
    chunk = width // slots
    core = lax.axis_index("c").astype(jnp.int32)
    depth = lax.axis_index("z").astype(jnp.int32)
    row = lax.axis_index("y").astype(jnp.int32)
    places = jnp.stack([core, depth, row])
    swap = [(0, 1), (1, 0)]
    product = 2 * width * tokens * HEAD
    token_bytes = 2 * tokens * width
    state_bytes = 4 * width * HEAD
    token_shape = jax.ShapeDtypeStruct((tokens, width), BF16)
    inner_shape = jax.ShapeDtypeStruct((tokens, width), F32)
    state_shape = jax.ShapeDtypeStruct((slots, chunk, HEAD), F32)
    chunk_shape = jax.ShapeDtypeStruct((chunk, HEAD), F32)
    inputs = (queries, key_row_matrix, value_row_matrix, output_gradient)

    keep, send = call(
        states_kernel,
        [SMEM] + [HBM] * 4,
        [VMEM] * 2,
        [state_shape] * 2,
        2 * product,
        4 * token_bytes + 2 * state_bytes,
        [
            pltpu.VMEM((4, LOADS, tokens, width // LOADS), BF16),
            pltpu.SemaphoreType.DMA((4, LOADS)),
        ],
    )(places, *(pltpu.with_memory_space_constraint(a, pltpu.HBM) for a in inputs))
    received = lax.ppermute(send, "c", swap)
    inner = call(
        inner_kernel,
        [VMEM] * 4,
        [VMEM] * 3,
        [inner_shape] * 3,
        5 * product,
        10 * token_bytes,
    )(*inputs)
    pieces = call(
        functools.partial(merge_kernel, order),
        [VMEM] * 2,
        [VMEM] * slots,
        [chunk_shape] * slots,
        width * HEAD,
        3 * state_bytes,
    )(keep, received)
    def total(*parts):
        return call(
            sum_kernel,
            [VMEM] * len(parts),
            VMEM,
            chunk_shape,
            len(parts) * chunk * HEAD,
            (len(parts) + 1) * 4 * chunk * HEAD,
        )(*parts)

    gathered = [p if k == 0 else turn(p, "z", slots, k) for k, p in zip(order, pieces, strict=True)]
    gathered, inner = lax.optimization_barrier((gathered, inner))
    column, keep = lax.optimization_barrier((total(*gathered), keep))
    other = lax.ppermute(keep, "c", swap)
    around = [turn(column, "y", rows, k) for k in range(1, rows)]
    around, other = lax.optimization_barrier((around, other))
    plane = total(column, *around)
    planes = [onward(plane, "x", sizes["x"], k) for k in range(1, sizes["x"])]
    prefixes = call(
        functools.partial(scan_kernel, order, rows),
        [SMEM] + [VMEM] * (slots + len(around) + len(planes)),
        [VMEM] * slots,
        [chunk_shape] * slots,
        2 * width * HEAD,
        3 * state_bytes,
        [pltpu.VMEM((slots, chunk, HEAD), F32)],
    )(places, *gathered, *around, *planes)
    own = [p if k == 0 else turn(p, "z", slots, k) for k, p in zip(order, prefixes, strict=True)]
    theirs = [lax.ppermute(part, "c", swap) for part in own]
    return call(
        functools.partial(outputs_kernel, order, scale),
        [SMEM] + [VMEM] * (8 + 2 * slots),
        [HBM] * 3,
        [token_shape] * 3,
        3 * product,
        13 * token_bytes + 3 * state_bytes,
        [
            pltpu.VMEM((3, slots, tokens, chunk), BF16),
            pltpu.SemaphoreType.DMA((3, slots)),
        ],
    )(places, *inputs, *inner, other, *own, *theirs)


def solution(mesh):
    sizes = {"y": 4, "z": 8, "c": 2, "x": 4}
    fine = Mesh(mesh.devices.reshape(tuple(sizes.values())), tuple(sizes))

    def program(queries, key_row_matrix, value_row_matrix, output_gradient):
        scale = float(HEAD * queries.shape[0]) ** -0.5
        spec = P(ROWS, None)
        return jax.shard_map(
            functools.partial(per_device, sizes, scale),
            mesh=fine,
            in_specs=(spec,) * 4,
            out_specs=(spec,) * 3,
            check_vma=False,
        )(queries, key_row_matrix, value_row_matrix, output_gradient)

    return program
```

```python
import functools

import jax
import jax.numpy as jnp
from jax import lax
from jax.experimental import pallas as pl
from jax.experimental.pallas import tpu as pltpu
from jax.sharding import Mesh
from jax.sharding import PartitionSpec as P

HEAD = 128
LOADS = 4
ROWS = ("x", "y", "z", "c")
SMEM = pl.BlockSpec(memory_space=pltpu.SMEM)
VMEM = pl.BlockSpec(memory_space=pltpu.VMEM)
HBM = pl.BlockSpec(memory_space=pltpu.HBM)
VMEM_LIMIT = 24 * 1024 * 1024
F32, BF16 = jnp.float32, jnp.bfloat16


def contract(lhs, rhs, lhs_dim, rhs_dim):
    return lax.dot_general(
        lhs, rhs, (((lhs_dim,), (rhs_dim,)), ((), ())), preferred_element_type=F32
    )


def chunk_lanes(index, width):
    return pl.ds(pl.multiple_of(index * width, width), width)


def moved(forward, place, step, count):
    return jnp.where(forward, lax.rem(place + step, count), lax.rem(place + count - step, count))


def states_kernel(places, query, key, value, gradient, keep, send, held, sems):
    first = places[0] == 0
    z = places[1]
    slots = keep.shape[0]
    width = keep.shape[1]
    part = held.shape[3]
    copies = []
    for n in range(held.shape[1]):
        for source, tensor in enumerate((key, value, query, gradient)):
            copy = pltpu.make_async_copy(
                tensor.at[:, pl.ds(n * part, part)], held.at[source, n], sems.at[source, n]
            )
            copy.start()
            copies.append(copy)
    for n in range(held.shape[1]):
        for copy in copies[4 * n : 4 * n + 4]:
            copy.wait()
        for h in range(part // HEAD):
            lanes = pl.ds(h * HEAD, HEAD)
            chunk, row = divmod(n * part + h * HEAD, width)
            ahead = lax.rem(chunk + slots - z, slots)
            behind = lax.rem(z + slots - chunk, slots)
            mine = jnp.where(first, ahead, behind)
            theirs = jnp.where(first, behind, ahead)
            kv = contract(held[0, n, :, lanes], held[1, n, :, lanes], 0, 0)
            qo = contract(held[2, n, :, lanes], held[3, n, :, lanes], 0, 0)
            keep[mine, pl.ds(row, HEAD), :] = jnp.where(first, kv, qo)
            send[theirs, pl.ds(row, HEAD), :] = jnp.where(first, qo, kv)


def inner_kernel(query, key, value, gradient, gq, gk, gv):
    count = query.shape[0]
    causal = lax.broadcasted_iota(jnp.int32, (count, count), 0) >= lax.broadcasted_iota(
        jnp.int32, (count, count), 1
    )
    for h in range(query.shape[1] // HEAD):
        lanes = pl.ds(h * HEAD, HEAD)
        q, k, v, g = query[:, lanes], key[:, lanes], value[:, lanes], gradient[:, lanes]
        dv = jnp.where(causal, contract(g, v, 1, 1), 0.0).astype(BF16)
        qk = jnp.where(causal, contract(q, k, 1, 1), 0.0).astype(BF16)
        gq[:, lanes] = contract(dv, k, 1, 0)
        gk[:, lanes] = contract(dv, q, 0, 0)
        gv[:, lanes] = contract(qk, g, 0, 0)


def merge_kernel(order, keep, received, *outs):
    for offset, out in zip(order, outs, strict=True):
        out[...] = keep[offset] + received[offset]


def sum_kernel(*refs):
    total = refs[0][...]
    for ref in refs[1:-1]:
        total = total + ref[...]
    refs[-1][...] = total


def scan_kernel(order, rows, places, *refs):
    slots = len(order)
    sources = refs[:slots]
    around = refs[slots : slots + rows - 1]
    planes = refs[slots + rows - 1 : -slots - 1]
    outs = refs[-slots - 1 : -1]
    held = refs[-1]
    first = places[0] == 0
    z = places[1]
    row = jnp.where(first, places[2], rows - 1 - places[2])
    total = planes[0][...]
    for plane in planes[1:]:
        total = total + plane[...]
    for step, part in enumerate(around, 1):
        total = total + jnp.where(row >= step, part[...], 0.0)
    for offset, source in zip(order, sources, strict=True):
        held[moved(first, z, slots - offset, slots)] = source[...]
    for n in range(slots):
        place = jnp.where(first, n, slots - 1 - n)
        piece = held[place]
        held[place] = total
        total = total + piece
    for offset, out in zip(order, outs, strict=True):
        out[...] = held[moved(first, z, offset, slots)]


def outputs_kernel(order, scale, places, *refs):
    slots = len(order)
    query, key, value, gradient = refs[:4]
    inner = refs[4:7]
    other = refs[7]
    own = refs[8 : 8 + slots]
    received = refs[8 + slots : 8 + 2 * slots]
    outs = refs[8 + 2 * slots : 11 + 2 * slots]
    held, sems = refs[11 + 2 * slots :]
    first = places[0] == 0
    z = places[1]
    width = own[0].shape[0]
    copies = []
    for n, offset in enumerate(order):
        chunk = moved(first, z, slots - offset, slots)
        mirror = order.index((slots - offset) % slots)
        for h in range(width // HEAD):
            rows = pl.ds(h * HEAD, HEAD)
            mine = own[n][rows, :]
            theirs = received[mirror][rows, :] + other[offset, rows, :]
            prefix = jnp.where(first, mine, theirs).astype(BF16)
            suffix = jnp.where(first, theirs, mine).astype(BF16)
            lanes = chunk_lanes(chunk * (width // HEAD) + h, HEAD)
            gq = contract(gradient[:, lanes], prefix, 1, 1)
            gk = contract(value[:, lanes], suffix, 1, 1)
            gv = contract(key[:, lanes], suffix, 1, 0)
            for t, result in enumerate((gq, gk, gv)):
                held[t, n, :, rows] = (scale * (result + inner[t][:, lanes])).astype(BF16)
        for t, out in enumerate(outs):
            copy = pltpu.make_async_copy(
                held.at[t, n], out.at[:, chunk_lanes(chunk, width)], sems.at[t, n]
            )
            copy.start()
            copies.append(copy)
    for copy in copies:
        copy.wait()


def call(kernel, in_specs, out_specs, out_shape, flops, moved, scratch=()):
    return pl.pallas_call(
        kernel,
        in_specs=in_specs,
        out_specs=out_specs,
        out_shape=out_shape,
        scratch_shapes=scratch,
        cost_estimate=pl.CostEstimate(flops=flops, bytes_accessed=moved, transcendentals=0),
        compiler_params=pltpu.CompilerParams(vmem_limit_bytes=VMEM_LIMIT),
    )


def turn(array, axis, count, step):
    steps = (step, count - step)
    pairs = [
        (2 * i + c, 2 * ((i + steps[c]) % count) + c) for i in range(count) for c in range(2)
    ]
    return lax.ppermute(array, (axis, "c"), pairs)


def onward(array, axis, count, step):
    pairs = [(i, i + step) for i in range(count - step)]
    pairs += [(count + i, count + i - step) for i in range(step, count)]
    return lax.ppermute(array, ("c", axis), pairs)


def issue_order(count):
    return sorted(range(count), key=lambda k: (k > 0, 2 * k != count, min(k, count - k), k))


def per_device(sizes, scale, queries, key_row_matrix, value_row_matrix, output_gradient):
    tokens, width = queries.shape
    slots = sizes["z"]
    rows = sizes["y"]
    order = issue_order(slots)
    chunk = width // slots
    core = lax.axis_index("c").astype(jnp.int32)
    depth = lax.axis_index("z").astype(jnp.int32)
    row = lax.axis_index("y").astype(jnp.int32)
    places = jnp.stack([core, depth, row])
    swap = [(0, 1), (1, 0)]
    product = 2 * width * tokens * HEAD
    token_bytes = 2 * tokens * width
    state_bytes = 4 * width * HEAD
    token_shape = jax.ShapeDtypeStruct((tokens, width), BF16)
    inner_shape = jax.ShapeDtypeStruct((tokens, width), F32)
    state_shape = jax.ShapeDtypeStruct((slots, chunk, HEAD), F32)
    chunk_shape = jax.ShapeDtypeStruct((chunk, HEAD), F32)
    inputs = (queries, key_row_matrix, value_row_matrix, output_gradient)

    keep, send = call(
        states_kernel,
        [SMEM] + [HBM] * 4,
        [VMEM] * 2,
        [state_shape] * 2,
        2 * product,
        4 * token_bytes + 2 * state_bytes,
        [
            pltpu.VMEM((4, LOADS, tokens, width // LOADS), BF16),
            pltpu.SemaphoreType.DMA((4, LOADS)),
        ],
    )(places, *(pltpu.with_memory_space_constraint(a, pltpu.HBM) for a in inputs))
    received = lax.ppermute(send, "c", swap)
    inner = call(
        inner_kernel,
        [VMEM] * 4,
        [VMEM] * 3,
        [inner_shape] * 3,
        5 * product,
        10 * token_bytes,
    )(*inputs)
    pieces = call(
        functools.partial(merge_kernel, order),
        [VMEM] * 2,
        [VMEM] * slots,
        [chunk_shape] * slots,
        width * HEAD,
        3 * state_bytes,
    )(keep, received)
    def total(*parts):
        return call(
            sum_kernel,
            [VMEM] * len(parts),
            VMEM,
            chunk_shape,
            len(parts) * chunk * HEAD,
            (len(parts) + 1) * 4 * chunk * HEAD,
        )(*parts)

    gathered = [p if k == 0 else turn(p, "z", slots, k) for k, p in zip(order, pieces, strict=True)]
    gathered, inner = lax.optimization_barrier((gathered, inner))
    column, keep = lax.optimization_barrier((total(*gathered), keep))
    other = lax.ppermute(keep, "c", swap)
    around = [turn(column, "y", rows, k) for k in range(1, rows)]
    around, other = lax.optimization_barrier((around, other))
    plane = total(column, *around)
    planes = [onward(plane, "x", sizes["x"], k) for k in range(1, sizes["x"])]
    prefixes = call(
        functools.partial(scan_kernel, order, rows),
        [SMEM] + [VMEM] * (slots + len(around) + len(planes)),
        [VMEM] * slots,
        [chunk_shape] * slots,
        2 * width * HEAD,
        3 * state_bytes,
        [pltpu.VMEM((slots, chunk, HEAD), F32)],
    )(places, *gathered, *around, *planes)
    own = [p if k == 0 else turn(p, "z", slots, k) for k, p in zip(order, prefixes, strict=True)]
    theirs = [lax.ppermute(part, "c", swap) for part in own]
    return call(
        functools.partial(outputs_kernel, order, scale),
        [SMEM] + [VMEM] * (8 + 2 * slots),
        [HBM] * 3,
        [token_shape] * 3,
        3 * product,
        13 * token_bytes + 3 * state_bytes,
        [
            pltpu.VMEM((3, slots, tokens, chunk), BF16),
            pltpu.SemaphoreType.DMA((3, slots)),
        ],
    )(places, *inputs, *inner, other, *own, *theirs)


def solution(mesh):
    sizes = {"y": 4, "z": 8, "c": 2, "x": 4}
    fine = Mesh(mesh.devices.reshape(tuple(sizes.values())), tuple(sizes))

    def program(queries, key_row_matrix, value_row_matrix, output_gradient):
        scale = float(HEAD * queries.shape[0]) ** -0.5
        spec = P(ROWS, None)
        return jax.shard_map(
            functools.partial(per_device, sizes, scale),
            mesh=fine,
            in_specs=(spec,) * 4,
            out_specs=(spec,) * 3,
            check_vma=False,
        )(queries, key_row_matrix, value_row_matrix, output_gradient)

    return program
```

```python
import functools

import jax
import jax.numpy as jnp
from jax import lax
from jax.experimental import pallas as pl
from jax.experimental.pallas import tpu as pltpu
from jax.sharding import Mesh
from jax.sharding import PartitionSpec as P

HEAD = 128
LOADS = 4
ROWS = ("x", "y", "z", "c")
SMEM = pl.BlockSpec(memory_space=pltpu.SMEM)
VMEM = pl.BlockSpec(memory_space=pltpu.VMEM)
HBM = pl.BlockSpec(memory_space=pltpu.HBM)
VMEM_LIMIT = 24 * 1024 * 1024
F32, BF16 = jnp.float32, jnp.bfloat16


def contract(lhs, rhs, lhs_dim, rhs_dim):
    return lax.dot_general(
        lhs, rhs, (((lhs_dim,), (rhs_dim,)), ((), ())), preferred_element_type=F32
    )


def states_kernel(places, query, key, value, gradient, keep, send, held, sems):
    first = places[0] == 0
    part = held.shape[3]
    copies = []
    for n in range(held.shape[1]):
        for source, tensor in enumerate((key, value, query, gradient)):
            copy = pltpu.make_async_copy(
                tensor.at[:, pl.ds(n * part, part)], held.at[source, n], sems.at[source, n]
            )
            copy.start()
            copies.append(copy)
    for n in range(held.shape[1]):
        for copy in copies[4 * n : 4 * n + 4]:
            copy.wait()
        for h in range(part // HEAD):
            lanes = pl.ds(h * HEAD, HEAD)
            rows = pl.ds(n * part + h * HEAD, HEAD)
            kv = contract(held[0, n, :, lanes], held[1, n, :, lanes], 0, 0)
            qo = contract(held[2, n, :, lanes], held[3, n, :, lanes], 0, 0)
            keep[rows, :] = jnp.where(first, kv, qo)
            send[rows, :] = jnp.where(first, qo, kv)


def inner_kernel(query, key, value, gradient, gq, gk, gv):
    count = query.shape[0]
    causal = lax.broadcasted_iota(jnp.int32, (count, count), 0) >= lax.broadcasted_iota(
        jnp.int32, (count, count), 1
    )
    for h in range(query.shape[1] // HEAD):
        lanes = pl.ds(h * HEAD, HEAD)
        q, k, v, g = query[:, lanes], key[:, lanes], value[:, lanes], gradient[:, lanes]
        dv = jnp.where(causal, contract(g, v, 1, 1), 0.0).astype(BF16)
        qk = jnp.where(causal, contract(q, k, 1, 1), 0.0).astype(BF16)
        gq[:, lanes] = contract(dv, k, 1, 0)
        gk[:, lanes] = contract(dv, q, 0, 0)
        gv[:, lanes] = contract(qk, g, 0, 0)


def merge_kernel(keep, received, out):
    out[...] = keep[...] + received[...]


def total_kernel(parts, out):
    total = parts[0]
    for n in range(1, parts.shape[0]):
        total = total + parts[n]
    out[...] = total


def scan_kernel(places, parts, *refs):
    first = places[0] == 0
    count = parts.shape[0]
    out = refs[-1]
    total = refs[0][...]
    for plane in refs[1:-1]:
        total = total + plane[...]
    for n in range(count):
        place = jnp.where(first, n, count - 1 - n)
        out[place] = total
        total = total + parts[place]


def outputs_kernel(scale, places, query, key, value, gradient, *refs):
    inner = refs[:3]
    other, own, received = refs[3:6]
    outs = refs[6:9]
    held, sems = refs[9:]
    first = places[0] == 0
    part = held.shape[3]
    copies = []
    for n in range(held.shape[1]):
        for h in range(part // HEAD):
            rows = pl.ds(n * part + h * HEAD, HEAD)
            mine = own[rows, :]
            theirs = received[rows, :] + other[rows, :]
            prefix = jnp.where(first, mine, theirs).astype(BF16)
            suffix = jnp.where(first, theirs, mine).astype(BF16)
            gq = contract(gradient[:, rows], prefix, 1, 1)
            gk = contract(value[:, rows], suffix, 1, 1)
            gv = contract(key[:, rows], suffix, 1, 0)
            for t, result in enumerate((gq, gk, gv)):
                held[t, n, :, pl.ds(h * HEAD, HEAD)] = (
                    scale * (result + inner[t][:, rows])
                ).astype(BF16)
        for t, out in enumerate(outs):
            copy = pltpu.make_async_copy(
                held.at[t, n], out.at[:, pl.ds(n * part, part)], sems.at[t, n]
            )
            copy.start()
            copies.append(copy)
    for copy in copies:
        copy.wait()


def call(kernel, in_specs, out_specs, out_shape, flops, moved, scratch=()):
    return pl.pallas_call(
        kernel,
        in_specs=in_specs,
        out_specs=out_specs,
        out_shape=out_shape,
        scratch_shapes=scratch,
        cost_estimate=pl.CostEstimate(flops=flops, bytes_accessed=moved, transcendentals=0),
        compiler_params=pltpu.CompilerParams(vmem_limit_bytes=VMEM_LIMIT),
    )


def onward(array, axis, count, step):
    pairs = [(i, i + step) for i in range(count - step)]
    pairs += [(count + i, count + i - step) for i in range(step, count)]
    return lax.ppermute(array, ("c", axis), pairs)


def per_device(sizes, scale, queries, key_row_matrix, value_row_matrix, output_gradient):
    tokens, width = queries.shape
    members = sizes["y"] * sizes["z"]
    places = lax.axis_index("c").astype(jnp.int32).reshape(1)
    swap = [(0, 1), (1, 0)]
    product = 2 * width * tokens * HEAD
    token_bytes = 2 * tokens * width
    state_bytes = 4 * width * HEAD
    token_shape = jax.ShapeDtypeStruct((tokens, width), BF16)
    inner_shape = jax.ShapeDtypeStruct((tokens, width), F32)
    state_shape = jax.ShapeDtypeStruct((width, HEAD), F32)
    parts_shape = jax.ShapeDtypeStruct((members, width // members, HEAD), F32)
    inputs = (queries, key_row_matrix, value_row_matrix, output_gradient)

    keep, send = call(
        states_kernel,
        [SMEM] + [HBM] * 4,
        [VMEM] * 2,
        [state_shape] * 2,
        2 * product,
        4 * token_bytes + 2 * state_bytes,
        [
            pltpu.VMEM((4, LOADS, tokens, width // LOADS), BF16),
            pltpu.SemaphoreType.DMA((4, LOADS)),
        ],
    )(places, *(pltpu.with_memory_space_constraint(a, pltpu.HBM) for a in inputs))
    received = lax.ppermute(send, "c", swap)
    chip = call(
        merge_kernel, [VMEM] * 2, VMEM, state_shape, width * HEAD, 3 * state_bytes
    )(keep, received)
    parts = lax.all_to_all(chip.reshape(parts_shape.shape), ("y", "z"), 0, 0, tiled=True)
    parts, keep, inputs = lax.optimization_barrier((parts, keep, inputs))
    plane = call(
        total_kernel,
        [VMEM],
        VMEM,
        jax.ShapeDtypeStruct(parts_shape.shape[1:], F32),
        width * HEAD,
        state_bytes,
    )(parts)
    planes = [onward(plane, "x", sizes["x"], k) for k in range(1, sizes["x"])]
    other = lax.ppermute(keep, "c", swap)
    inner = call(
        inner_kernel,
        [VMEM] * 4,
        [VMEM] * 3,
        [inner_shape] * 3,
        5 * product,
        10 * token_bytes,
    )(*inputs)
    planes, other, inner = lax.optimization_barrier((planes, other, inner))
    prefixes = call(
        scan_kernel,
        [SMEM] + [VMEM] * (1 + len(planes)),
        VMEM,
        parts_shape,
        width * HEAD,
        2 * state_bytes,
    )(places, parts, *planes)
    own = lax.all_to_all(prefixes, ("y", "z"), 0, 0, tiled=True).reshape(width, HEAD)
    theirs = lax.ppermute(own, "c", swap)
    return call(
        functools.partial(outputs_kernel, scale),
        [SMEM] + [VMEM] * 10,
        [HBM] * 3,
        [token_shape] * 3,
        3 * product,
        13 * token_bytes + 3 * state_bytes,
        [
            pltpu.VMEM((3, LOADS, tokens, width // LOADS), BF16),
            pltpu.SemaphoreType.DMA((3, LOADS)),
        ],
    )(places, *inputs, *inner, other, own, theirs)


def solution(mesh):
    sizes = {"y": 4, "z": 8, "c": 2, "x": 4}
    fine = Mesh(mesh.devices.reshape(tuple(sizes.values())), tuple(sizes))

    def program(queries, key_row_matrix, value_row_matrix, output_gradient):
        scale = float(HEAD * queries.shape[0]) ** -0.5
        spec = P(ROWS, None)
        return jax.shard_map(
            functools.partial(per_device, sizes, scale),
            mesh=fine,
            in_specs=(spec,) * 4,
            out_specs=(spec,) * 3,
            check_vma=False,
        )(queries, key_row_matrix, value_row_matrix, output_gradient)

    return program
```

```python
import functools

import jax
import jax.numpy as jnp
from jax import lax
from jax.experimental import pallas as pl
from jax.experimental.pallas import tpu as pltpu
from jax.sharding import Mesh
from jax.sharding import PartitionSpec as P

HEAD = 128
LOADS = 4
EARLY = 10
ROWS = ("x", "y", "z", "c")
SMEM = pl.BlockSpec(memory_space=pltpu.SMEM)
VMEM = pl.BlockSpec(memory_space=pltpu.VMEM)
HBM = pl.BlockSpec(memory_space=pltpu.HBM)
VMEM_LIMIT = 24 * 1024 * 1024
F32, BF16 = jnp.float32, jnp.bfloat16


def contract(lhs, rhs, lhs_dim, rhs_dim):
    return lax.dot_general(
        lhs, rhs, (((lhs_dim,), (rhs_dim,)), ((), ())), preferred_element_type=F32
    )


def states_kernel(places, query, key, value, gradient, q, k, v, g, keep, send, sems):
    first = places[0] == 0
    loads = sems.shape[1]
    part = query.shape[1] // loads
    pairs = ((key, k), (value, v), (query, q), (gradient, g))
    copies = []
    for n in range(loads):
        lanes = pl.ds(n * part, part)
        for t, (source, target) in enumerate(pairs):
            copy = pltpu.make_async_copy(source.at[:, lanes], target.at[:, lanes], sems.at[t, n])
            copy.start()
            copies.append(copy)
    for n in range(loads):
        for copy in copies[4 * n : 4 * n + 4]:
            copy.wait()
        for h in range(part // HEAD):
            rows = pl.ds(n * part + h * HEAD, HEAD)
            kv = contract(k[:, rows], v[:, rows], 0, 0)
            qo = contract(q[:, rows], g[:, rows], 0, 0)
            keep[rows, :] = jnp.where(first, kv, qo)
            send[rows, :] = jnp.where(first, qo, kv)


def inner_kernel(base, query, key, value, gradient, gq, gk, gv):
    count = query.shape[0]
    causal = lax.broadcasted_iota(jnp.int32, (count, count), 0) >= lax.broadcasted_iota(
        jnp.int32, (count, count), 1
    )
    for h in range(gq.shape[1] // HEAD):
        lanes = pl.ds(base + h * HEAD, HEAD)
        q, k, v, g = query[:, lanes], key[:, lanes], value[:, lanes], gradient[:, lanes]
        dv = jnp.where(causal, contract(g, v, 1, 1), 0.0).astype(BF16)
        qk = jnp.where(causal, contract(q, k, 1, 1), 0.0).astype(BF16)
        lanes = pl.ds(h * HEAD, HEAD)
        gq[:, lanes] = contract(dv, k, 1, 0)
        gk[:, lanes] = contract(dv, q, 0, 0)
        gv[:, lanes] = contract(qk, g, 0, 0)


def merge_kernel(keep, received, out):
    out[...] = keep[...] + received[...]


def total_kernel(parts, out):
    total = parts[0]
    for n in range(1, parts.shape[0]):
        total = total + parts[n]
    out[...] = total


def scan_kernel(places, parts, *refs):
    first = places[0] == 0
    count = parts.shape[0]
    out = refs[-1]
    total = refs[0][...]
    for plane in refs[1:-1]:
        total = total + plane[...]
    for n in range(count):
        place = jnp.where(first, n, count - 1 - n)
        out[place] = total
        total = total + parts[place]


def outputs_kernel(scale, whose, places, query, key, value, gradient, *refs):
    inner = (refs[:3], refs[3:6])
    states = refs[6:-5]
    outs = refs[-5:-2]
    held, sems = refs[-2:]
    loads = sems.shape[1]
    part = query.shape[1] // loads
    cut = inner[0][0].shape[1]

    def state(rows):
        total = states[0][rows, :]
        if whose:
            total = total + states[1][rows, :]
        return total.astype(BF16)

    def produce(tensors):
        copies = []
        for n in range(loads):
            for h in range(part // HEAD):
                at = n * part + h * HEAD
                lanes = pl.ds(at, HEAD)
                group, lane = (0, at) if at < cut else (1, at - cut)
                summed = state(lanes)
                for t in tensors:
                    source, dim = ((gradient, 1), (value, 1), (key, 0))[t]
                    result = contract(source[:, lanes], summed, 1, dim)
                    result = result + inner[group][t][:, pl.ds(lane, HEAD)]
                    held[t, n, :, pl.ds(h * HEAD, HEAD)] = (scale * result).astype(BF16)
            for t in tensors:
                copy = pltpu.make_async_copy(
                    held.at[t, n], outs[t].at[:, pl.ds(n * part, part)], sems.at[t, n]
                )
                copy.start()
                copies.append(copy)
        for copy in copies:
            copy.wait()

    @pl.when(places[0] == whose)
    def _():
        produce((0,))

    @pl.when(places[0] != whose)
    def _():
        produce((1, 2))


def call(kernel, in_specs, out_specs, out_shape, flops, moved, scratch=(), aliases=None):
    return pl.pallas_call(
        kernel,
        in_specs=in_specs,
        out_specs=out_specs,
        out_shape=out_shape,
        scratch_shapes=scratch,
        input_output_aliases=aliases or {},
        cost_estimate=pl.CostEstimate(flops=flops, bytes_accessed=moved, transcendentals=0),
        compiler_params=pltpu.CompilerParams(vmem_limit_bytes=VMEM_LIMIT),
    )


def onward(array, axis, count, step):
    pairs = [(i, i + step) for i in range(count - step)]
    pairs += [(count + i, count + i - step) for i in range(step, count)]
    return lax.ppermute(array, ("c", axis), pairs)


def per_device(sizes, scale, queries, key_row_matrix, value_row_matrix, output_gradient):
    tokens, width = queries.shape
    members = sizes["y"] * sizes["z"]
    places = lax.axis_index("c").astype(jnp.int32).reshape(1)
    swap = [(0, 1), (1, 0)]
    product = 2 * width * tokens * HEAD
    token_bytes = 2 * tokens * width
    state_bytes = 4 * width * HEAD
    token_shape = jax.ShapeDtypeStruct((tokens, width), BF16)
    state_shape = jax.ShapeDtypeStruct((width, HEAD), F32)
    parts_shape = jax.ShapeDtypeStruct((members, width // members, HEAD), F32)
    inputs = (queries, key_row_matrix, value_row_matrix, output_gradient)

    *inputs, keep, send = call(
        states_kernel,
        [SMEM] + [HBM] * 4,
        [VMEM] * 6,
        [token_shape] * 4 + [state_shape] * 2,
        2 * product,
        8 * token_bytes + 2 * state_bytes,
        [pltpu.SemaphoreType.DMA((4, LOADS))],
    )(places, *(pltpu.with_memory_space_constraint(a, pltpu.HBM) for a in inputs))

    def inner(base, span):
        return call(
            functools.partial(inner_kernel, base),
            [VMEM] * 4,
            [VMEM] * 3,
            [jax.ShapeDtypeStruct((tokens, span), F32)] * 3,
            5 * product * span // width,
            10 * token_bytes * span // width,
        )(*inputs)

    received = lax.ppermute(send, "c", swap)
    early = inner(0, EARLY * HEAD)
    received, early = lax.optimization_barrier((received, early))
    chip = call(
        merge_kernel, [VMEM] * 2, VMEM, state_shape, width * HEAD, 3 * state_bytes
    )(keep, received)
    parts = lax.all_to_all(chip.reshape(parts_shape.shape), ("y", "z"), 0, 0, tiled=True)
    parts, keep, inputs = lax.optimization_barrier((parts, keep, inputs))
    plane = call(
        total_kernel,
        [VMEM],
        VMEM,
        jax.ShapeDtypeStruct(parts_shape.shape[1:], F32),
        width * HEAD,
        state_bytes,
    )(parts)
    planes = [onward(plane, "x", sizes["x"], k) for k in range(1, sizes["x"])]
    other = lax.ppermute(keep, "c", swap)
    late = inner(EARLY * HEAD, width - EARLY * HEAD)
    planes, other, late = lax.optimization_barrier((planes, other, late))
    prefixes = call(
        scan_kernel,
        [SMEM] + [VMEM] * (1 + len(planes)),
        VMEM,
        parts_shape,
        width * HEAD,
        2 * state_bytes,
    )(places, parts, *planes)
    own = lax.all_to_all(prefixes, ("y", "z"), 0, 0, tiled=True).reshape(width, HEAD)
    theirs = lax.ppermute(own, "c", swap)

    def outputs(whose, states, results):
        return call(
            functools.partial(outputs_kernel, scale, whose),
            [SMEM] + [VMEM] * (10 + len(states)) + [HBM] * len(results),
            [HBM] * 3,
            [token_shape] * 3,
            3 * product // 2,
            7 * token_bytes + 2 * state_bytes,
            [
                pltpu.VMEM((3, LOADS, tokens, width // LOADS), BF16),
                pltpu.SemaphoreType.DMA((3, LOADS)),
            ],
            {11 + len(states) + n: n for n in range(len(results))},
        )(places, *inputs, *early, *late, *states, *results)

    results = outputs(0, (own,), ())
    return tuple(outputs(1, (theirs, other), tuple(results)))


def solution(mesh):
    sizes = {"y": 4, "z": 8, "c": 2, "x": 4}
    fine = Mesh(mesh.devices.reshape(tuple(sizes.values())), tuple(sizes))

    def program(queries, key_row_matrix, value_row_matrix, output_gradient):
        scale = float(HEAD * queries.shape[0]) ** -0.5
        spec = P(ROWS, None)
        return jax.shard_map(
            functools.partial(per_device, sizes, scale),
            mesh=fine,
            in_specs=(spec,) * 4,
            out_specs=(spec,) * 3,
            check_vma=False,
        )(queries, key_row_matrix, value_row_matrix, output_gradient)

    return program
```

```python
import functools

import jax
import jax.numpy as jnp
from jax import lax
from jax.experimental import pallas as pl
from jax.experimental.pallas import tpu as pltpu
from jax.sharding import Mesh
from jax.sharding import PartitionSpec as P

HEAD = 128
LOADS = 4
EARLY = 10
ROWS = ("x", "y", "z", "c")
SMEM = pl.BlockSpec(memory_space=pltpu.SMEM)
VMEM = pl.BlockSpec(memory_space=pltpu.VMEM)
HBM = pl.BlockSpec(memory_space=pltpu.HBM)
VMEM_LIMIT = 24 * 1024 * 1024
F32, BF16 = jnp.float32, jnp.bfloat16


def contract(lhs, rhs, lhs_dim, rhs_dim):
    return lax.dot_general(
        lhs, rhs, (((lhs_dim,), (rhs_dim,)), ((), ())), preferred_element_type=F32
    )


def states_kernel(places, query, key, value, gradient, q, k, v, g, keep, send, sems):
    first = places[0] == 0
    loads = sems.shape[1]
    part = query.shape[1] // loads
    pairs = ((key, k), (value, v), (query, q), (gradient, g))
    copies = []
    for n in range(loads):
        lanes = pl.ds(n * part, part)
        for t, (source, target) in enumerate(pairs):
            copy = pltpu.make_async_copy(source.at[:, lanes], target.at[:, lanes], sems.at[t, n])
            copy.start()
            copies.append(copy)
    for n in range(loads):
        for copy in copies[4 * n : 4 * n + 4]:
            copy.wait()
        for h in range(part // HEAD):
            rows = pl.ds(n * part + h * HEAD, HEAD)
            kv = contract(k[:, rows], v[:, rows], 0, 0)
            qo = contract(q[:, rows], g[:, rows], 0, 0)
            keep[rows, :] = jnp.where(first, kv, qo)
            send[rows, :] = jnp.where(first, qo, kv)


def inner_kernel(base, query, key, value, gradient, gq, gk, gv):
    count = query.shape[0]
    causal = lax.broadcasted_iota(jnp.int32, (count, count), 0) >= lax.broadcasted_iota(
        jnp.int32, (count, count), 1
    )
    for h in range(gq.shape[1] // HEAD):
        lanes = pl.ds(base + h * HEAD, HEAD)
        q, k, v, g = query[:, lanes], key[:, lanes], value[:, lanes], gradient[:, lanes]
        dv = jnp.where(causal, contract(g, v, 1, 1), 0.0).astype(BF16)
        qk = jnp.where(causal, contract(q, k, 1, 1), 0.0).astype(BF16)
        lanes = pl.ds(h * HEAD, HEAD)
        gq[:, lanes] = contract(dv, k, 1, 0)
        gk[:, lanes] = contract(dv, q, 0, 0)
        gv[:, lanes] = contract(qk, g, 0, 0)


def merge_kernel(keep, received, out):
    out[...] = keep[...] + received[...]


def total_kernel(parts, out):
    total = parts[0]
    for n in range(1, parts.shape[0]):
        total = total + parts[n]
    out[...] = total


def scan_kernel(order, places, parts, *refs):
    first = places[0] == 0
    count = parts.shape[0]
    out = refs[-1]
    total = refs[0][...]
    for plane in refs[1:-1]:
        total = total + plane[...]
    for n in range(count):
        place = jnp.where(first, order[n], order[count - 1 - n])
        out[place] = total
        total = total + parts[place]


def outputs_kernel(scale, whose, places, query, key, value, gradient, *refs):
    inner = (refs[:3], refs[3:6])
    states = refs[6:-5]
    outs = refs[-5:-2]
    held, sems = refs[-2:]
    loads = sems.shape[1]
    part = query.shape[1] // loads
    cut = inner[0][0].shape[1]

    def state(rows):
        return states[0][rows, :].astype(BF16)

    def produce(tensors):
        copies = []
        for n in range(loads):
            for h in range(part // HEAD):
                at = n * part + h * HEAD
                lanes = pl.ds(at, HEAD)
                group, lane = (0, at) if at < cut else (1, at - cut)
                summed = state(lanes)
                for t in tensors:
                    source, dim = ((gradient, 1), (value, 1), (key, 0))[t]
                    result = contract(source[:, lanes], summed, 1, dim)
                    result = result + inner[group][t][:, pl.ds(lane, HEAD)]
                    held[t, n, :, pl.ds(h * HEAD, HEAD)] = (scale * result).astype(BF16)
            for t in tensors:
                copy = pltpu.make_async_copy(
                    held.at[t, n], outs[t].at[:, pl.ds(n * part, part)], sems.at[t, n]
                )
                copy.start()
                copies.append(copy)
        for copy in copies:
            copy.wait()

    @pl.when(places[0] == whose)
    def _():
        produce((0,))

    @pl.when(places[0] != whose)
    def _():
        produce((1, 2))


def call(kernel, in_specs, out_specs, out_shape, flops, moved, scratch=(), aliases=None):
    return pl.pallas_call(
        kernel,
        in_specs=in_specs,
        out_specs=out_specs,
        out_shape=out_shape,
        scratch_shapes=scratch,
        input_output_aliases=aliases or {},
        cost_estimate=pl.CostEstimate(flops=flops, bytes_accessed=moved, transcendentals=0),
        compiler_params=pltpu.CompilerParams(vmem_limit_bytes=VMEM_LIMIT),
    )


def order_of(sizes):
    rows, depths = sizes["y"], sizes["z"]
    last = rows * depths - 1
    return [last - (n % depths * rows + n // depths) for n in range(last + 1)]


def exchange(sizes, array):
    order = order_of(sizes)
    members = sorted(range(len(order)), key=lambda n: order[n])
    groups = [
        [(n * sizes["c"] + c) * sizes["x"] + x for n in members]
        for c in range(sizes["c"])
        for x in range(sizes["x"])
    ]
    return lax.all_to_all(
        array, tuple(sizes), 0, 0, tiled=True, axis_index_groups=groups
    )


def onward(array, axis, count, step):
    pairs = [(i, i + step) for i in range(count - step)]
    pairs += [(count + i, count + i - step) for i in range(step, count)]
    return lax.ppermute(array, ("c", axis), pairs)


def per_device(sizes, scale, queries, key_row_matrix, value_row_matrix, output_gradient):
    tokens, width = queries.shape
    members = sizes["y"] * sizes["z"]
    places = lax.axis_index("c").astype(jnp.int32).reshape(1)
    swap = [(0, 1), (1, 0)]
    product = 2 * width * tokens * HEAD
    token_bytes = 2 * tokens * width
    state_bytes = 4 * width * HEAD
    token_shape = jax.ShapeDtypeStruct((tokens, width), BF16)
    state_shape = jax.ShapeDtypeStruct((width, HEAD), F32)
    parts_shape = jax.ShapeDtypeStruct((members, width // members, HEAD), F32)
    inputs = (queries, key_row_matrix, value_row_matrix, output_gradient)

    *inputs, keep, send = call(
        states_kernel,
        [SMEM] + [HBM] * 4,
        [VMEM] * 6,
        [token_shape] * 4 + [state_shape] * 2,
        2 * product,
        8 * token_bytes + 2 * state_bytes,
        [pltpu.SemaphoreType.DMA((4, LOADS))],
    )(places, *(pltpu.with_memory_space_constraint(a, pltpu.HBM) for a in inputs))

    def inner(base, span):
        return call(
            functools.partial(inner_kernel, base),
            [VMEM] * 4,
            [VMEM] * 3,
            [jax.ShapeDtypeStruct((tokens, span), F32)] * 3,
            5 * product * span // width,
            10 * token_bytes * span // width,
        )(*inputs)

    received = lax.ppermute(send, "c", swap)
    early = inner(0, EARLY * HEAD)
    received, early = lax.optimization_barrier((received, early))
    chip = call(
        merge_kernel, [VMEM] * 2, VMEM, state_shape, width * HEAD, 3 * state_bytes
    )(keep, received)
    parts = exchange(sizes, chip.reshape(parts_shape.shape))
    parts, inputs = lax.optimization_barrier((parts, inputs))
    plane = call(
        total_kernel,
        [VMEM],
        VMEM,
        jax.ShapeDtypeStruct(parts_shape.shape[1:], F32),
        width * HEAD,
        state_bytes,
    )(parts)
    planes = [onward(plane, "x", sizes["x"], k) for k in range(1, sizes["x"])]
    late = inner(EARLY * HEAD, width - EARLY * HEAD)
    planes, late = lax.optimization_barrier((planes, late))
    prefixes = call(
        functools.partial(scan_kernel, order_of(sizes)),
        [SMEM] + [VMEM] * (1 + len(planes)),
        VMEM,
        parts_shape,
        width * HEAD,
        2 * state_bytes,
    )(places, parts, *planes)
    own = exchange(sizes, prefixes).reshape(width, HEAD)
    onto = call(
        merge_kernel, [VMEM] * 2, VMEM, state_shape, width * HEAD, 3 * state_bytes
    )(own, keep)
    theirs = lax.ppermute(onto, "c", swap)

    def outputs(whose, states, results):
        return call(
            functools.partial(outputs_kernel, scale, whose),
            [SMEM] + [VMEM] * (10 + len(states)) + [HBM] * len(results),
            [HBM] * 3,
            [token_shape] * 3,
            3 * product // 2,
            7 * token_bytes + 2 * state_bytes,
            [
                pltpu.VMEM((3, LOADS, tokens, width // LOADS), BF16),
                pltpu.SemaphoreType.DMA((3, LOADS)),
            ],
            {11 + len(states) + n: n for n in range(len(results))},
        )(places, *inputs, *early, *late, *states, *results)

    results = outputs(0, (own,), ())
    return tuple(outputs(1, (theirs,), tuple(results)))


def solution(mesh):
    sizes = {"y": 4, "z": 8, "c": 2, "x": 4}
    fine = Mesh(mesh.devices.reshape(tuple(sizes.values())), tuple(sizes))

    def program(queries, key_row_matrix, value_row_matrix, output_gradient):
        scale = float(HEAD * queries.shape[0]) ** -0.5
        spec = P(ROWS, None)
        return jax.shard_map(
            functools.partial(per_device, sizes, scale),
            mesh=fine,
            in_specs=(spec,) * 4,
            out_specs=(spec,) * 3,
            check_vma=False,
        )(queries, key_row_matrix, value_row_matrix, output_gradient)

    return program
```

```python
import functools

import jax
import jax.numpy as jnp
from jax import lax
from jax.experimental import pallas as pl
from jax.experimental.pallas import tpu as pltpu
from jax.sharding import Mesh
from jax.sharding import PartitionSpec as P

HEAD = 128
LOADS = 4
ROWS = ("x", "y", "z", "c")
SMEM = pl.BlockSpec(memory_space=pltpu.SMEM)
VMEM = pl.BlockSpec(memory_space=pltpu.VMEM)
HBM = pl.BlockSpec(memory_space=pltpu.HBM)
VMEM_LIMIT = 24 * 1024 * 1024
F32, BF16 = jnp.float32, jnp.bfloat16


def contract(lhs, rhs, lhs_dim, rhs_dim):
    return lax.dot_general(
        lhs, rhs, (((lhs_dim,), (rhs_dim,)), ((), ())), preferred_element_type=F32
    )


def load(pairs, sems):
    loads = sems.shape[1]
    width = pairs[0][0].shape[1] // loads
    copies = []
    for n in range(loads):
        lanes = pl.ds(n * width, width)
        for t, (source, target) in enumerate(pairs):
            copy = pltpu.make_async_copy(source.at[:, lanes], target.at[:, lanes], sems.at[t, n])
            copy.start()
            copies.append(copy)
    return copies


def states(pairs, sems, out):
    copies = load(pairs, sems)
    lhs, rhs = (target for _, target in pairs)
    loads = sems.shape[1]
    span = lhs.shape[1] // loads
    for n in range(loads):
        for copy in copies[2 * n : 2 * n + 2]:
            copy.wait()
        for h in range(span // HEAD):
            rows = pl.ds(n * span + h * HEAD, HEAD)
            out[rows, :] = contract(lhs[:, rows], rhs[:, rows], 0, 0)


def send_kernel(core, query, key, value, gradient, send, left, right, sems):
    @pl.when(core[0] == 0)
    def _():
        states(((query, left), (gradient, right)), sems, send)

    @pl.when(core[0] != 0)
    def _():
        states(((key, left), (value, right)), sems, send)


def keep_kernel(core, query, key, value, gradient, keep, q, k, v, g, sems, more):
    @pl.when(core[0] == 0)
    def _():
        rest = load(((query, q), (gradient, g)), more)
        states(((key, k), (value, v)), sems, keep)
        for copy in rest:
            copy.wait()

    @pl.when(core[0] != 0)
    def _():
        rest = load(((key, k), (value, v)), more)
        states(((query, q), (gradient, g)), sems, keep)
        for copy in rest:
            copy.wait()


def inner_products(query, key, value, gradient, gq, gk, gv):
    count = query.shape[0]
    causal = lax.broadcasted_iota(jnp.int32, (count, count), 0) >= lax.broadcasted_iota(
        jnp.int32, (count, count), 1
    )
    for h in range(query.shape[1] // HEAD):
        lanes = pl.ds(h * HEAD, HEAD)
        q, k, v, g = query[:, lanes], key[:, lanes], value[:, lanes], gradient[:, lanes]
        dv = jnp.where(causal, contract(g, v, 1, 1), 0.0).astype(BF16)
        qk = jnp.where(causal, contract(q, k, 1, 1), 0.0).astype(BF16)
        gq[:, lanes] = contract(dv, k, 1, 0)
        gk[:, lanes] = contract(dv, q, 0, 0)
        gv[:, lanes] = contract(qk, g, 0, 0)


def merge_kernel(core, keep, received, *refs):
    @pl.when(core[0] == 0)
    def _():
        inner_products(*refs[:4], *refs[5:])

    refs[4][...] = keep[...] + received[...]


def onto_kernel(core, own, keep, *refs):
    @pl.when(core[0] != 0)
    def _():
        inner_products(*refs[:4], *refs[8:])

    refs[7][...] = own[...] + keep[...]


def total_kernel(parts, out):
    total = parts[0]
    for n in range(1, parts.shape[0]):
        total = total + parts[n]
    out[...] = total


def scan_kernel(order, places, parts, *refs):
    first = places[0] == 0
    count = parts.shape[0]
    out = refs[-1]
    total = refs[0][...]
    for plane in refs[1:-1]:
        total = total + plane[...]
    for n in range(count):
        place = jnp.where(first, order[n], order[count - 1 - n])
        out[place] = total
        total = total + parts[place]


def outputs_kernel(scale, whose, places, query, key, value, gradient, *refs):
    inner = refs[:3]
    sums = refs[3:-5]
    outs = refs[-5:-2]
    held, sems = refs[-2:]
    loads = sems.shape[1]
    part = query.shape[1] // loads

    def state(rows):
        return sums[0][rows, :].astype(BF16)

    def produce(tensors):
        copies = []
        for n in range(loads):
            for h in range(part // HEAD):
                at = n * part + h * HEAD
                lanes = pl.ds(at, HEAD)
                summed = state(lanes)
                for t in tensors:
                    source, dim = ((gradient, 1), (value, 1), (key, 0))[t]
                    result = contract(source[:, lanes], summed, 1, dim)
                    result = result + inner[t][:, lanes]
                    held[t, n, :, pl.ds(h * HEAD, HEAD)] = (scale * result).astype(BF16)
            for t in tensors:
                copy = pltpu.make_async_copy(
                    held.at[t, n], outs[t].at[:, pl.ds(n * part, part)], sems.at[t, n]
                )
                copy.start()
                copies.append(copy)
        for copy in copies:
            copy.wait()

    @pl.when(places[0] == whose)
    def _():
        produce((0,))

    @pl.when(places[0] != whose)
    def _():
        produce((1, 2))


def call(kernel, in_specs, out_specs, out_shape, flops, moved, scratch=(), aliases=None):
    return pl.pallas_call(
        kernel,
        in_specs=in_specs,
        out_specs=out_specs,
        out_shape=out_shape,
        scratch_shapes=scratch,
        input_output_aliases=aliases or {},
        cost_estimate=pl.CostEstimate(flops=flops, bytes_accessed=moved, transcendentals=0),
        compiler_params=pltpu.CompilerParams(vmem_limit_bytes=VMEM_LIMIT),
    )


def order_of(sizes):
    rows, depths = sizes["y"], sizes["z"]
    last = rows * depths - 1
    return [last - (n % depths * rows + n // depths) for n in range(last + 1)]


def exchange(sizes, array):
    order = order_of(sizes)
    members = sorted(range(len(order)), key=lambda n: order[n])
    groups = [
        [(n * sizes["c"] + c) * sizes["x"] + x for n in members]
        for c in range(sizes["c"])
        for x in range(sizes["x"])
    ]
    return lax.all_to_all(
        array, tuple(sizes), 0, 0, tiled=True, axis_index_groups=groups
    )


def onward(array, axis, count, step):
    pairs = [(i, i + step) for i in range(count - step)]
    pairs += [(count + i, count + i - step) for i in range(step, count)]
    return lax.ppermute(array, ("c", axis), pairs)


def per_device(sizes, scale, queries, key_row_matrix, value_row_matrix, output_gradient):
    tokens, width = queries.shape
    members = sizes["y"] * sizes["z"]
    places = lax.axis_index("c").astype(jnp.int32).reshape(1)
    swap = [(0, 1), (1, 0)]
    product = 2 * width * tokens * HEAD
    token_bytes = 2 * tokens * width
    state_bytes = 4 * width * HEAD
    token_shape = jax.ShapeDtypeStruct((tokens, width), BF16)
    state_shape = jax.ShapeDtypeStruct((width, HEAD), F32)
    parts_shape = jax.ShapeDtypeStruct((members, width // members, HEAD), F32)
    inputs = (queries, key_row_matrix, value_row_matrix, output_gradient)

    inner_shape = jax.ShapeDtypeStruct((tokens, width), F32)
    resting = [pltpu.with_memory_space_constraint(a, pltpu.HBM) for a in inputs]
    send = call(
        send_kernel,
        [SMEM] + [HBM] * 4,
        VMEM,
        state_shape,
        product,
        2 * token_bytes + state_bytes,
        [pltpu.VMEM((tokens, width), BF16)] * 2 + [pltpu.SemaphoreType.DMA((2, LOADS))],
    )(places, *resting)
    received = lax.ppermute(send, "c", swap)
    keep, *inputs = call(
        keep_kernel,
        [SMEM] + [HBM] * 4,
        [VMEM] * 5,
        [state_shape] + [token_shape] * 4,
        product,
        8 * token_bytes + state_bytes,
        [pltpu.SemaphoreType.DMA((2, LOADS))] * 2,
    )(places, *resting)
    received, keep = lax.optimization_barrier((received, keep))
    chip, *inner = call(
        merge_kernel,
        [SMEM] + [VMEM] * 6,
        [VMEM] * 4,
        [state_shape] + [inner_shape] * 3,
        5 * product,
        10 * token_bytes + 3 * state_bytes,
    )(places, keep, received, *inputs)
    parts = exchange(sizes, chip.reshape(parts_shape.shape))
    plane = call(
        total_kernel,
        [VMEM],
        VMEM,
        jax.ShapeDtypeStruct(parts_shape.shape[1:], F32),
        width * HEAD,
        state_bytes,
    )(parts)
    planes = [onward(plane, "x", sizes["x"], k) for k in range(1, sizes["x"])]
    prefixes = call(
        functools.partial(scan_kernel, order_of(sizes)),
        [SMEM] + [VMEM] * (1 + len(planes)),
        VMEM,
        parts_shape,
        width * HEAD,
        2 * state_bytes,
    )(places, parts, *planes)
    own = exchange(sizes, prefixes).reshape(width, HEAD)
    onto, *inner = call(
        onto_kernel,
        [SMEM] + [VMEM] * 9,
        [VMEM] * 4,
        [state_shape] + [inner_shape] * 3,
        5 * product,
        10 * token_bytes + 3 * state_bytes,
        aliases={7 + n: 1 + n for n in range(3)},
    )(places, own, keep, *inputs, *inner)
    theirs = lax.ppermute(onto, "c", swap)

    def outputs(whose, states, results):
        return call(
            functools.partial(outputs_kernel, scale, whose),
            [SMEM] + [VMEM] * (7 + len(states)) + [HBM] * len(results),
            [HBM] * 3,
            [token_shape] * 3,
            3 * product // 2,
            7 * token_bytes + 2 * state_bytes,
            [
                pltpu.VMEM((3, LOADS, tokens, width // LOADS), BF16),
                pltpu.SemaphoreType.DMA((3, LOADS)),
            ],
            {8 + len(states) + n: n for n in range(len(results))},
        )(places, *inputs, *inner, *states, *results)

    results = outputs(0, (own,), ())
    return tuple(outputs(1, (theirs,), tuple(results)))


def solution(mesh):
    sizes = {"y": 4, "z": 8, "c": 2, "x": 4}
    fine = Mesh(mesh.devices.reshape(tuple(sizes.values())), tuple(sizes))

    def program(queries, key_row_matrix, value_row_matrix, output_gradient):
        scale = float(HEAD * queries.shape[0]) ** -0.5
        spec = P(ROWS, None)
        return jax.shard_map(
            functools.partial(per_device, sizes, scale),
            mesh=fine,
            in_specs=(spec,) * 4,
            out_specs=(spec,) * 3,
            check_vma=False,
        )(queries, key_row_matrix, value_row_matrix, output_gradient)

    return program
```

```python
import functools

import jax
import jax.numpy as jnp
from jax import lax
from jax.experimental import pallas as pl
from jax.experimental.pallas import tpu as pltpu
from jax.sharding import Mesh
from jax.sharding import PartitionSpec as P

HEAD = 128
LOADS = 2
ROWS = ("x", "y", "z", "c")
SMEM = pl.BlockSpec(memory_space=pltpu.SMEM)
VMEM = pl.BlockSpec(memory_space=pltpu.VMEM)
HBM = pl.BlockSpec(memory_space=pltpu.HBM)
VMEM_LIMIT = 24 * 1024 * 1024
F32, BF16 = jnp.float32, jnp.bfloat16


def contract(lhs, rhs, lhs_dim, rhs_dim):
    return lax.dot_general(
        lhs, rhs, (((lhs_dim,), (rhs_dim,)), ((), ())), preferred_element_type=F32
    )


def load(pairs, sems):
    loads = sems.shape[1]
    width = pairs[0][0].shape[1] // loads
    copies = []
    for n in range(loads):
        lanes = pl.ds(n * width, width)
        for t, (source, target) in enumerate(pairs):
            copy = pltpu.make_async_copy(source.at[:, lanes], target.at[:, lanes], sems.at[t, n])
            copy.start()
            copies.append(copy)
    return copies


def states(pairs, sems, out):
    copies = load(pairs, sems)
    lhs, rhs = (target for _, target in pairs)
    loads = sems.shape[1]
    span = lhs.shape[1] // loads
    for n in range(loads):
        for copy in copies[2 * n : 2 * n + 2]:
            copy.wait()
        for h in range(span // HEAD):
            rows = pl.ds(n * span + h * HEAD, HEAD)
            out[rows, :] = contract(lhs[:, rows], rhs[:, rows], 0, 0)


def send_kernel(core, query, key, value, gradient, send, left, right, sems):
    @pl.when(lax.rem(core[0], 2) == 0)
    def _():
        states(((query, left), (gradient, right)), sems, send)

    @pl.when(lax.rem(core[0], 2) != 0)
    def _():
        states(((key, left), (value, right)), sems, send)


def keep_kernel(core, query, key, value, gradient, keep, q, k, v, g, sems, more):
    @pl.when(lax.rem(core[0], 2) == 0)
    def _():
        rest = load(((query, q), (gradient, g)), more)
        states(((key, k), (value, v)), sems, keep)
        for copy in rest:
            copy.wait()

    @pl.when(lax.rem(core[0], 2) != 0)
    def _():
        rest = load(((key, k), (value, v)), more)
        states(((query, q), (gradient, g)), sems, keep)
        for copy in rest:
            copy.wait()


def inner_products(query, key, value, gradient, gq, gk, gv):
    count = query.shape[0]
    causal = lax.broadcasted_iota(jnp.int32, (count, count), 0) >= lax.broadcasted_iota(
        jnp.int32, (count, count), 1
    )
    for h in range(query.shape[1] // HEAD):
        lanes = pl.ds(h * HEAD, HEAD)
        q, k, v, g = query[:, lanes], key[:, lanes], value[:, lanes], gradient[:, lanes]
        dv = jnp.where(causal, contract(g, v, 1, 1), 0.0).astype(BF16)
        qk = jnp.where(causal, contract(q, k, 1, 1), 0.0).astype(BF16)
        gq[:, lanes] = contract(dv, k, 1, 0)
        gk[:, lanes] = contract(dv, q, 0, 0)
        gv[:, lanes] = contract(qk, g, 0, 0)


def merge_kernel(core, keep, received, *refs):
    @pl.when(lax.rem(core[0], 2) == 0)
    def _():
        inner_products(*refs[:4], *refs[5:])

    refs[4][...] = keep[...] + received[...]


def onto_kernel(core, own, keep, *refs):
    @pl.when(lax.rem(core[0], 2) != 0)
    def _():
        inner_products(*refs[:4], *refs[8:])

    refs[7][...] = own[...] + keep[...]


def total_kernel(parts, out):
    total = parts[0]
    for n in range(1, parts.shape[0]):
        total = total + parts[n]
    out[...] = total


def scan_kernel(order, places, parts, *refs):
    first = lax.rem(places[0], 2) == 0
    count = parts.shape[0]
    out = refs[-1]
    spot = lax.div(places[0], 2)
    spot = jnp.where(first, spot, len(refs) - 1 - spot)
    total = jnp.zeros(out.shape[1:], F32)
    for step, plane in enumerate(refs[:-1], 1):
        total = total + jnp.where(spot >= step, plane[...], 0.0)
    for n in range(count):
        place = jnp.where(first, order[n], order[count - 1 - n])
        out[place] = total
        total = total + parts[place]


def outputs_kernel(scale, whose, places, query, key, value, gradient, *refs):
    inner = refs[:3]
    sums = refs[3:-5]
    outs = refs[-5:-2]
    held, sems = refs[-2:]
    loads = sems.shape[1]
    part = query.shape[1] // loads

    def state(rows):
        return sums[0][rows, :].astype(BF16)

    def produce(tensors):
        copies = []
        for n in range(loads):
            for h in range(part // HEAD):
                at = n * part + h * HEAD
                lanes = pl.ds(at, HEAD)
                summed = state(lanes)
                for t in tensors:
                    source, dim = ((gradient, 1), (value, 1), (key, 0))[t]
                    result = contract(source[:, lanes], summed, 1, dim)
                    result = result + inner[t][:, lanes]
                    held[t, n, :, pl.ds(h * HEAD, HEAD)] = (scale * result).astype(BF16)
            for t in tensors:
                copy = pltpu.make_async_copy(
                    held.at[t, n], outs[t].at[:, pl.ds(n * part, part)], sems.at[t, n]
                )
                copy.start()
                copies.append(copy)
        for copy in copies:
            copy.wait()

    @pl.when(lax.rem(places[0], 2) == whose)
    def _():
        produce((0,))

    @pl.when(lax.rem(places[0], 2) != whose)
    def _():
        produce((1, 2))


def call(kernel, in_specs, out_specs, out_shape, flops, moved, scratch=(), aliases=None):
    return pl.pallas_call(
        kernel,
        in_specs=in_specs,
        out_specs=out_specs,
        out_shape=out_shape,
        scratch_shapes=scratch,
        input_output_aliases=aliases or {},
        cost_estimate=pl.CostEstimate(flops=flops, bytes_accessed=moved, transcendentals=0),
        compiler_params=pltpu.CompilerParams(vmem_limit_bytes=VMEM_LIMIT),
    )


def order_of(sizes):
    rows, depths = sizes["y"], sizes["z"]
    last = rows * depths - 1
    return [17 * (last - (n % depths * rows + n // depths)) % (last + 1) for n in range(last + 1)]


def exchange(sizes, array):
    order = order_of(sizes)
    members = sorted(range(len(order)), key=lambda n: order[n])
    groups = [
        [(n * sizes["c"] + c) * sizes["x"] + x for n in members]
        for c in range(sizes["c"])
        for x in range(sizes["x"])
    ]
    return lax.all_to_all(
        array, tuple(sizes), 0, 0, tiled=True, axis_index_groups=groups
    )


def onward(array, axis, count, step):
    pairs = [(i, (i + step) % count) for i in range(count)]
    pairs += [(count + i, count + (i - step) % count) for i in range(count)]
    return lax.ppermute(array, ("c", axis), pairs)


def per_device(sizes, scale, queries, key_row_matrix, value_row_matrix, output_gradient):
    tokens, width = queries.shape
    members = sizes["y"] * sizes["z"]
    places = lax.axis_index("c") + 2 * lax.axis_index("x")
    places = places.astype(jnp.int32).reshape(1)
    swap = [(0, 1), (1, 0)]
    product = 2 * width * tokens * HEAD
    token_bytes = 2 * tokens * width
    state_bytes = 4 * width * HEAD
    token_shape = jax.ShapeDtypeStruct((tokens, width), BF16)
    state_shape = jax.ShapeDtypeStruct((width, HEAD), F32)
    parts_shape = jax.ShapeDtypeStruct((members, width // members, HEAD), F32)
    inputs = (queries, key_row_matrix, value_row_matrix, output_gradient)

    inner_shape = jax.ShapeDtypeStruct((tokens, width), F32)
    resting = [pltpu.with_memory_space_constraint(a, pltpu.HBM) for a in inputs]
    send = call(
        send_kernel,
        [SMEM] + [HBM] * 4,
        VMEM,
        state_shape,
        product,
        2 * token_bytes + state_bytes,
        [pltpu.VMEM((tokens, width), BF16)] * 2 + [pltpu.SemaphoreType.DMA((2, LOADS))],
    )(places, *resting)
    received = lax.ppermute(send, "c", swap)
    keep, *inputs = call(
        keep_kernel,
        [SMEM] + [HBM] * 4,
        [VMEM] * 5,
        [state_shape] + [token_shape] * 4,
        product,
        8 * token_bytes + state_bytes,
        [pltpu.SemaphoreType.DMA((2, LOADS))] * 2,
    )(places, *resting)
    received, keep = lax.optimization_barrier((received, keep))
    chip, *inner = call(
        merge_kernel,
        [SMEM] + [VMEM] * 6,
        [VMEM] * 4,
        [state_shape] + [inner_shape] * 3,
        5 * product,
        10 * token_bytes + 3 * state_bytes,
    )(places, keep, received, *inputs)
    parts = exchange(sizes, chip.reshape(parts_shape.shape))
    plane = call(
        total_kernel,
        [VMEM],
        VMEM,
        jax.ShapeDtypeStruct(parts_shape.shape[1:], F32),
        width * HEAD,
        state_bytes,
    )(parts)
    planes = [onward(plane, "x", sizes["x"], k) for k in range(1, sizes["x"])]
    prefixes = call(
        functools.partial(scan_kernel, order_of(sizes)),
        [SMEM] + [VMEM] * (1 + len(planes)),
        VMEM,
        parts_shape,
        width * HEAD,
        2 * state_bytes,
    )(places, parts, *planes)
    own = exchange(sizes, prefixes).reshape(width, HEAD)
    onto, *inner = call(
        onto_kernel,
        [SMEM] + [VMEM] * 9,
        [VMEM] * 4,
        [state_shape] + [inner_shape] * 3,
        5 * product,
        10 * token_bytes + 3 * state_bytes,
        aliases={7 + n: 1 + n for n in range(3)},
    )(places, own, keep, *inputs, *inner)
    theirs = lax.ppermute(onto, "c", swap)

    def outputs(whose, states, results):
        return call(
            functools.partial(outputs_kernel, scale, whose),
            [SMEM] + [VMEM] * (7 + len(states)) + [HBM] * len(results),
            [HBM] * 3,
            [token_shape] * 3,
            3 * product // 2,
            7 * token_bytes + 2 * state_bytes,
            [
                pltpu.VMEM((3, LOADS, tokens, width // LOADS), BF16),
                pltpu.SemaphoreType.DMA((3, LOADS)),
            ],
            {8 + len(states) + n: n for n in range(len(results))},
        )(places, *inputs, *inner, *states, *results)

    results = outputs(0, (own,), ())
    return tuple(outputs(1, (theirs,), tuple(results)))


def solution(mesh):
    sizes = {"y": 4, "z": 8, "c": 2, "x": 4}
    fine = Mesh(mesh.devices.reshape(tuple(sizes.values())), tuple(sizes))

    def program(queries, key_row_matrix, value_row_matrix, output_gradient):
        scale = float(HEAD * queries.shape[0]) ** -0.5
        spec = P(ROWS, None)
        return jax.shard_map(
            functools.partial(per_device, sizes, scale),
            mesh=fine,
            in_specs=(spec,) * 4,
            out_specs=(spec,) * 3,
            check_vma=False,
        )(queries, key_row_matrix, value_row_matrix, output_gradient)

    return program
```

```python
import functools

import jax
import jax.numpy as jnp
from jax import lax
from jax.experimental import pallas as pl
from jax.experimental.pallas import tpu as pltpu
from jax.sharding import Mesh
from jax.sharding import PartitionSpec as P

HEAD = 128
LOADS = 2
ROWS = ("x", "y", "z", "c")
SMEM = pl.BlockSpec(memory_space=pltpu.SMEM)
VMEM = pl.BlockSpec(memory_space=pltpu.VMEM)
HBM = pl.BlockSpec(memory_space=pltpu.HBM)
VMEM_LIMIT = 24 * 1024 * 1024
F32, BF16 = jnp.float32, jnp.bfloat16


def contract(lhs, rhs, lhs_dim, rhs_dim):
    return lax.dot_general(
        lhs, rhs, (((lhs_dim,), (rhs_dim,)), ((), ())), preferred_element_type=F32
    )


def load(pairs, sems):
    loads = sems.shape[1]
    width = pairs[0][0].shape[1] // loads
    copies = []
    for n in range(loads):
        lanes = pl.ds(n * width, width)
        for t, (source, target) in enumerate(pairs):
            copy = pltpu.make_async_copy(source.at[:, lanes], target.at[:, lanes], sems.at[t, n])
            copy.start()
            copies.append(copy)
    return copies


def states(pairs, sems, out):
    copies = load(pairs, sems)
    lhs, rhs = (target for _, target in pairs)
    loads = sems.shape[1]
    span = lhs.shape[1] // loads
    for n in range(loads):
        for copy in copies[2 * n : 2 * n + 2]:
            copy.wait()
        for h in range(span // HEAD):
            rows = pl.ds(n * span + h * HEAD, HEAD)
            out[rows, :] = contract(lhs[:, rows], rhs[:, rows], 0, 0)


def send_kernel(core, query, key, value, gradient, send, left, right, sems):
    @pl.when(lax.rem(core[0], 2) == 0)
    def _():
        states(((query, left), (gradient, right)), sems, send)

    @pl.when(lax.rem(core[0], 2) != 0)
    def _():
        states(((key, left), (value, right)), sems, send)


def keep_kernel(core, query, key, value, gradient, keep, q, k, v, g, sems, more):
    @pl.when(lax.rem(core[0], 2) != 0)
    def _():
        rest = load(((key, k), (value, v)), more)
        states(((query, q), (gradient, g)), sems, keep)
        for copy in rest:
            copy.wait()


def inner_products(query, key, value, gradient, gq, gk, gv):
    count = query.shape[0]
    causal = lax.broadcasted_iota(jnp.int32, (count, count), 0) >= lax.broadcasted_iota(
        jnp.int32, (count, count), 1
    )
    for h in range(query.shape[1] // HEAD):
        lanes = pl.ds(h * HEAD, HEAD)
        q, k, v, g = query[:, lanes], key[:, lanes], value[:, lanes], gradient[:, lanes]
        dv = jnp.where(causal, contract(g, v, 1, 1), 0.0).astype(BF16)
        qk = jnp.where(causal, contract(q, k, 1, 1), 0.0).astype(BF16)
        gq[:, lanes] = contract(dv, k, 1, 0)
        gk[:, lanes] = contract(dv, q, 0, 0)
        gv[:, lanes] = contract(qk, g, 0, 0)


def merge_kernel(core, query, key, value, gradient, received, *refs):
    keep, q, k, v, g, chip = refs[5:11]
    inner, sems, more = refs[11:14], refs[14], refs[15]

    @pl.when(lax.rem(core[0], 2) == 0)
    def _():
        rest = load(((query, q), (gradient, g)), more)
        states(((key, k), (value, v)), sems, keep)
        for copy in rest:
            copy.wait()
        inner_products(q, k, v, g, *inner)
        chip[...] = keep[...] + received[...]

    @pl.when(lax.rem(core[0], 2) != 0)
    def _():
        chip[...] = refs[0][...] + received[...]


def onto_kernel(core, own, keep, *refs):
    @pl.when(lax.rem(core[0], 2) != 0)
    def _():
        inner_products(*refs[:4], *refs[8:])

    refs[7][...] = own[...] + keep[...]


def total_kernel(parts, out):
    total = parts[0]
    for n in range(1, parts.shape[0]):
        total = total + parts[n]
    out[...] = total


def scan_kernel(order, places, parts, *refs):
    first = lax.rem(places[0], 2) == 0
    count = parts.shape[0]
    out = refs[-1]
    spot = lax.div(places[0], 2)
    spot = jnp.where(first, spot, len(refs) - 1 - spot)
    total = jnp.zeros(out.shape[1:], F32)
    for step, plane in enumerate(refs[:-1], 1):
        total = total + jnp.where(spot >= step, plane[...], 0.0)
    for n in range(count):
        place = jnp.where(first, order[n], order[count - 1 - n])
        out[place] = total
        total = total + parts[place]


def outputs_kernel(scale, whose, places, query, key, value, gradient, *refs):
    inner = refs[:3]
    sums = refs[3:-5]
    outs = refs[-5:-2]
    held, sems = refs[-2:]
    loads = sems.shape[1]
    part = query.shape[1] // loads

    def state(rows):
        return sums[0][rows, :].astype(BF16)

    def produce(tensors):
        copies = []
        for n in range(loads):
            for h in range(part // HEAD):
                at = n * part + h * HEAD
                lanes = pl.ds(at, HEAD)
                summed = state(lanes)
                for t in tensors:
                    source, dim = ((gradient, 1), (value, 1), (key, 0))[t]
                    result = contract(source[:, lanes], summed, 1, dim)
                    result = result + inner[t][:, lanes]
                    held[t, n, :, pl.ds(h * HEAD, HEAD)] = (scale * result).astype(BF16)
            for t in tensors:
                copy = pltpu.make_async_copy(
                    held.at[t, n], outs[t].at[:, pl.ds(n * part, part)], sems.at[t, n]
                )
                copy.start()
                copies.append(copy)
        for copy in copies:
            copy.wait()

    @pl.when(lax.rem(places[0], 2) == whose)
    def _():
        produce((0,))

    @pl.when(lax.rem(places[0], 2) != whose)
    def _():
        produce((1, 2))


def call(kernel, in_specs, out_specs, out_shape, flops, moved, scratch=(), aliases=None):
    return pl.pallas_call(
        kernel,
        in_specs=in_specs,
        out_specs=out_specs,
        out_shape=out_shape,
        scratch_shapes=scratch,
        input_output_aliases=aliases or {},
        cost_estimate=pl.CostEstimate(flops=flops, bytes_accessed=moved, transcendentals=0),
        compiler_params=pltpu.CompilerParams(vmem_limit_bytes=VMEM_LIMIT),
    )


def order_of(sizes):
    rows, depths = sizes["y"], sizes["z"]
    last = rows * depths - 1
    return [17 * (last - (n % depths * rows + n // depths)) % (last + 1) for n in range(last + 1)]


def exchange(sizes, array):
    order = order_of(sizes)
    members = sorted(range(len(order)), key=lambda n: order[n])
    groups = [
        [(n * sizes["c"] + c) * sizes["x"] + x for n in members]
        for c in range(sizes["c"])
        for x in range(sizes["x"])
    ]
    return lax.all_to_all(
        array, tuple(sizes), 0, 0, tiled=True, axis_index_groups=groups
    )


def onward(array, axis, count, step):
    pairs = [(i, (i + step) % count) for i in range(count)]
    pairs += [(count + i, count + (i - step) % count) for i in range(count)]
    return lax.ppermute(array, ("c", axis), pairs)


def per_device(sizes, scale, queries, key_row_matrix, value_row_matrix, output_gradient):
    tokens, width = queries.shape
    members = sizes["y"] * sizes["z"]
    places = lax.axis_index("c") + 2 * lax.axis_index("x")
    places = places.astype(jnp.int32).reshape(1)
    swap = [(0, 1), (1, 0)]
    product = 2 * width * tokens * HEAD
    token_bytes = 2 * tokens * width
    state_bytes = 4 * width * HEAD
    token_shape = jax.ShapeDtypeStruct((tokens, width), BF16)
    state_shape = jax.ShapeDtypeStruct((width, HEAD), F32)
    parts_shape = jax.ShapeDtypeStruct((members, width // members, HEAD), F32)
    inputs = (queries, key_row_matrix, value_row_matrix, output_gradient)

    inner_shape = jax.ShapeDtypeStruct((tokens, width), F32)
    resting = [pltpu.with_memory_space_constraint(a, pltpu.HBM) for a in inputs]
    send = call(
        send_kernel,
        [SMEM] + [HBM] * 4,
        VMEM,
        state_shape,
        product,
        2 * token_bytes + state_bytes,
        [pltpu.VMEM((tokens, width), BF16)] * 2 + [pltpu.SemaphoreType.DMA((2, LOADS))],
    )(places, *resting)
    received = lax.ppermute(send, "c", swap)
    keep, *inputs = call(
        keep_kernel,
        [SMEM] + [HBM] * 4,
        [VMEM] * 5,
        [state_shape] + [token_shape] * 4,
        product,
        8 * token_bytes + state_bytes,
        [pltpu.SemaphoreType.DMA((2, LOADS))] * 2,
    )(places, *resting)
    received, keep = lax.optimization_barrier((received, keep))
    keep, *rest = call(
        merge_kernel,
        [SMEM] + [HBM] * 4 + [VMEM] * 6,
        [VMEM] * 9,
        [state_shape] + [token_shape] * 4 + [state_shape] + [inner_shape] * 3,
        6 * product,
        14 * token_bytes + 3 * state_bytes,
        [pltpu.SemaphoreType.DMA((2, LOADS))] * 2,
        {6 + n: n for n in range(5)},
    )(places, *resting, received, keep, *inputs)
    inputs, chip, inner = rest[:4], rest[4], rest[5:]
    parts = exchange(sizes, chip.reshape(parts_shape.shape))
    plane = call(
        total_kernel,
        [VMEM],
        VMEM,
        jax.ShapeDtypeStruct(parts_shape.shape[1:], F32),
        width * HEAD,
        state_bytes,
    )(parts)
    planes = [onward(plane, "x", sizes["x"], k) for k in range(1, sizes["x"])]
    prefixes = call(
        functools.partial(scan_kernel, order_of(sizes)),
        [SMEM] + [VMEM] * (1 + len(planes)),
        VMEM,
        parts_shape,
        width * HEAD,
        2 * state_bytes,
    )(places, parts, *planes)
    own = exchange(sizes, prefixes).reshape(width, HEAD)
    onto, *inner = call(
        onto_kernel,
        [SMEM] + [VMEM] * 9,
        [VMEM] * 4,
        [state_shape] + [inner_shape] * 3,
        5 * product,
        10 * token_bytes + 3 * state_bytes,
        aliases={7 + n: 1 + n for n in range(3)},
    )(places, own, keep, *inputs, *inner)
    theirs = lax.ppermute(onto, "c", swap)

    def outputs(whose, states, results):
        return call(
            functools.partial(outputs_kernel, scale, whose),
            [SMEM] + [VMEM] * (7 + len(states)) + [HBM] * len(results),
            [HBM] * 3,
            [token_shape] * 3,
            3 * product // 2,
            7 * token_bytes + 2 * state_bytes,
            [
                pltpu.VMEM((3, LOADS, tokens, width // LOADS), BF16),
                pltpu.SemaphoreType.DMA((3, LOADS)),
            ],
            {8 + len(states) + n: n for n in range(len(results))},
        )(places, *inputs, *inner, *states, *results)

    results = outputs(0, (own,), ())
    return tuple(outputs(1, (theirs,), tuple(results)))


def solution(mesh):
    sizes = {"y": 4, "z": 8, "c": 2, "x": 4}
    fine = Mesh(mesh.devices.reshape(tuple(sizes.values())), tuple(sizes))

    def program(queries, key_row_matrix, value_row_matrix, output_gradient):
        scale = float(HEAD * queries.shape[0]) ** -0.5
        spec = P(ROWS, None)
        return jax.shard_map(
            functools.partial(per_device, sizes, scale),
            mesh=fine,
            in_specs=(spec,) * 4,
            out_specs=(spec,) * 3,
            check_vma=False,
        )(queries, key_row_matrix, value_row_matrix, output_gradient)

    return program
```

```python
import functools

import jax
import jax.numpy as jnp
from jax import lax
from jax.experimental import pallas as pl
from jax.experimental.pallas import tpu as pltpu
from jax.sharding import Mesh
from jax.sharding import PartitionSpec as P

HEAD = 128
LOADS = 2
STORES = 4
ROWS = ("x", "y", "z", "c")
SMEM = pl.BlockSpec(memory_space=pltpu.SMEM)
VMEM = pl.BlockSpec(memory_space=pltpu.VMEM)
HBM = pl.BlockSpec(memory_space=pltpu.HBM)
VMEM_LIMIT = 24 * 1024 * 1024
F32, BF16 = jnp.float32, jnp.bfloat16


def contract(lhs, rhs, lhs_dim, rhs_dim):
    return lax.dot_general(
        lhs, rhs, (((lhs_dim,), (rhs_dim,)), ((), ())), preferred_element_type=F32
    )


def load(pairs, sems):
    loads = sems.shape[1]
    width = pairs[0][0].shape[1] // loads
    copies = []
    for n in range(loads):
        lanes = pl.ds(n * width, width)
        for t, (source, target) in enumerate(pairs):
            copy = pltpu.make_async_copy(source.at[:, lanes], target.at[:, lanes], sems.at[t, n])
            copy.start()
            copies.append(copy)
    return copies


def states(pairs, sems, out):
    copies = load(pairs, sems)
    lhs, rhs = (target for _, target in pairs)
    loads = sems.shape[1]
    span = lhs.shape[1] // loads
    for n in range(loads):
        for copy in copies[2 * n : 2 * n + 2]:
            copy.wait()
        for h in range(span // HEAD):
            rows = pl.ds(n * span + h * HEAD, HEAD)
            out[rows, :] = contract(lhs[:, rows], rhs[:, rows], 0, 0)


def send_kernel(core, query, key, value, gradient, send, left, right, sems):
    @pl.when(lax.rem(core[0], 2) == 0)
    def _():
        states(((query, left), (gradient, right)), sems, send)

    @pl.when(lax.rem(core[0], 2) != 0)
    def _():
        states(((value, left), (key, right)), sems, send)


def keep_kernel(core, query, key, value, gradient, keep, q, k, v, g, sems, more):
    @pl.when(lax.rem(core[0], 2) != 0)
    def _():
        rest = load(((key, k), (value, v)), more)
        states(((query, q), (gradient, g)), sems, keep)
        for copy in rest:
            copy.wait()


def inner_products(query, key, value, gradient, gq, gk, gv):
    count = query.shape[0]
    causal = lax.broadcasted_iota(jnp.int32, (count, count), 0) >= lax.broadcasted_iota(
        jnp.int32, (count, count), 1
    )
    for h in range(query.shape[1] // HEAD):
        lanes = pl.ds(h * HEAD, HEAD)
        q, k, v, g = query[:, lanes], key[:, lanes], value[:, lanes], gradient[:, lanes]
        dv = jnp.where(causal, contract(g, v, 1, 1), 0.0).astype(BF16)
        qk = jnp.where(causal, contract(q, k, 1, 1), 0.0).astype(BF16)
        gq[:, lanes] = contract(dv, k, 1, 0)
        gk[:, lanes] = contract(dv, q, 0, 0)
        gv[:, lanes] = contract(qk, g, 0, 0)


def merge_kernel(core, query, key, value, gradient, received, *refs):
    keep, q, k, v, g, chip = refs[5:11]
    inner, sems, more = refs[11:14], refs[14], refs[15]

    @pl.when(lax.rem(core[0], 2) == 0)
    def _():
        rest = load(((query, q), (gradient, g)), more)
        states(((value, v), (key, k)), sems, keep)
        for copy in rest:
            copy.wait()
        inner_products(q, k, v, g, *inner)
        chip[...] = keep[...] + received[...]

    @pl.when(lax.rem(core[0], 2) != 0)
    def _():
        chip[...] = refs[0][...] + received[...]


def onto_kernel(core, own, keep, *refs):
    @pl.when(lax.rem(core[0], 2) != 0)
    def _():
        inner_products(*refs[:4], *refs[8:])

    refs[7][...] = own[...] + keep[...]


def total_kernel(parts, out):
    total = parts[0]
    for n in range(1, parts.shape[0]):
        total = total + parts[n]
    out[...] = total


def scan_kernel(order, places, parts, *refs):
    first = lax.rem(places[0], 2) == 0
    count = parts.shape[0]
    out = refs[-1]
    spot = lax.div(places[0], 2)
    spot = jnp.where(first, spot, len(refs) - 1 - spot)
    total = jnp.zeros(out.shape[1:], F32)
    for step, plane in enumerate(refs[:-1], 1):
        total = total + jnp.where(spot >= step, plane[...], 0.0)
    for n in range(count):
        place = jnp.where(first, order[n], order[count - 1 - n])
        out[place] = total
        total = total + parts[place]


def outputs_kernel(scale, whose, places, query, key, value, gradient, *refs):
    inner = refs[:3]
    sums = refs[3:-5]
    outs = refs[-5:-2]
    held, sems = refs[-2:]
    loads = sems.shape[1]
    part = query.shape[1] // loads

    def state(rows):
        return sums[0][rows, :].astype(BF16)

    def produce(tensors):
        copies = []
        for n in range(loads):
            for h in range(part // HEAD):
                at = n * part + h * HEAD
                lanes = pl.ds(at, HEAD)
                summed = state(lanes)
                for t in tensors:
                    source, dim = ((gradient, 0), (value, 1), (key, 0))[t]
                    result = contract(source[:, lanes], summed, 1, dim)
                    result = result + inner[t][:, lanes]
                    held[t, n, :, pl.ds(h * HEAD, HEAD)] = (scale * result).astype(BF16)
            for t in tensors:
                copy = pltpu.make_async_copy(
                    held.at[t, n], outs[t].at[:, pl.ds(n * part, part)], sems.at[t, n]
                )
                copy.start()
                copies.append(copy)
        for copy in copies:
            copy.wait()

    @pl.when(lax.rem(places[0], 2) == whose)
    def _():
        produce((0,))

    @pl.when(lax.rem(places[0], 2) != whose)
    def _():
        produce((1, 2))


def call(kernel, in_specs, out_specs, out_shape, flops, moved, scratch=(), aliases=None):
    return pl.pallas_call(
        kernel,
        in_specs=in_specs,
        out_specs=out_specs,
        out_shape=out_shape,
        scratch_shapes=scratch,
        input_output_aliases=aliases or {},
        cost_estimate=pl.CostEstimate(flops=flops, bytes_accessed=moved, transcendentals=0),
        compiler_params=pltpu.CompilerParams(vmem_limit_bytes=VMEM_LIMIT),
    )


def order_of(sizes):
    rows, depths = sizes["y"], sizes["z"]
    last = rows * depths - 1
    return [17 * (last - (n % depths * rows + n // depths)) % (last + 1) for n in range(last + 1)]


def exchange(sizes, array):
    order = order_of(sizes)
    members = sorted(range(len(order)), key=lambda n: order[n])
    groups = [
        [(n * sizes["c"] + c) * sizes["x"] + x for n in members]
        for c in range(sizes["c"])
        for x in range(sizes["x"])
    ]
    return lax.all_to_all(
        array, tuple(sizes), 0, 0, tiled=True, axis_index_groups=groups
    )


def onward(array, axis, count, step):
    pairs = [(i, (i + step) % count) for i in range(count)]
    pairs += [(count + i, count + (i - step) % count) for i in range(count)]
    return lax.ppermute(array, ("c", axis), pairs)


def per_device(sizes, scale, queries, key_row_matrix, value_row_matrix, output_gradient):
    tokens, width = queries.shape
    members = sizes["y"] * sizes["z"]
    places = lax.axis_index("c") + 2 * lax.axis_index("x")
    places = places.astype(jnp.int32).reshape(1)
    swap = [(0, 1), (1, 0)]
    product = 2 * width * tokens * HEAD
    token_bytes = 2 * tokens * width
    state_bytes = 4 * width * HEAD
    token_shape = jax.ShapeDtypeStruct((tokens, width), BF16)
    state_shape = jax.ShapeDtypeStruct((width, HEAD), F32)
    parts_shape = jax.ShapeDtypeStruct((members, width // members, HEAD), F32)
    inputs = (queries, key_row_matrix, value_row_matrix, output_gradient)

    inner_shape = jax.ShapeDtypeStruct((tokens, width), F32)
    resting = [pltpu.with_memory_space_constraint(a, pltpu.HBM) for a in inputs]
    send = call(
        send_kernel,
        [SMEM] + [HBM] * 4,
        VMEM,
        state_shape,
        product,
        2 * token_bytes + state_bytes,
        [pltpu.VMEM((tokens, width), BF16)] * 2 + [pltpu.SemaphoreType.DMA((2, LOADS))],
    )(places, *resting)
    received = lax.ppermute(send, "c", swap)
    keep, *inputs = call(
        keep_kernel,
        [SMEM] + [HBM] * 4,
        [VMEM] * 5,
        [state_shape] + [token_shape] * 4,
        product,
        8 * token_bytes + state_bytes,
        [pltpu.SemaphoreType.DMA((2, LOADS))] * 2,
    )(places, *resting)
    received, keep = lax.optimization_barrier((received, keep))
    keep, *rest = call(
        merge_kernel,
        [SMEM] + [HBM] * 4 + [VMEM] * 6,
        [VMEM] * 9,
        [state_shape] + [token_shape] * 4 + [state_shape] + [inner_shape] * 3,
        6 * product,
        14 * token_bytes + 3 * state_bytes,
        [pltpu.SemaphoreType.DMA((2, LOADS))] * 2,
        {6 + n: n for n in range(5)},
    )(places, *resting, received, keep, *inputs)
    inputs, chip, inner = rest[:4], rest[4], rest[5:]
    parts = exchange(sizes, chip.reshape(parts_shape.shape))
    plane = call(
        total_kernel,
        [VMEM],
        VMEM,
        jax.ShapeDtypeStruct(parts_shape.shape[1:], F32),
        width * HEAD,
        state_bytes,
    )(parts)
    planes = [onward(plane, "x", sizes["x"], k) for k in range(1, sizes["x"])]
    prefixes = call(
        functools.partial(scan_kernel, order_of(sizes)),
        [SMEM] + [VMEM] * (1 + len(planes)),
        VMEM,
        parts_shape,
        width * HEAD,
        2 * state_bytes,
    )(places, parts, *planes)
    own = exchange(sizes, prefixes).reshape(width, HEAD)
    onto, *inner = call(
        onto_kernel,
        [SMEM] + [VMEM] * 9,
        [VMEM] * 4,
        [state_shape] + [inner_shape] * 3,
        5 * product,
        10 * token_bytes + 3 * state_bytes,
        aliases={7 + n: 1 + n for n in range(3)},
    )(places, own, keep, *inputs, *inner)
    theirs = lax.ppermute(onto, "c", swap)

    def outputs(whose, states, results):
        return call(
            functools.partial(outputs_kernel, scale, whose),
            [SMEM] + [VMEM] * (7 + len(states)) + [HBM] * len(results),
            [HBM] * 3,
            [token_shape] * 3,
            3 * product // 2,
            7 * token_bytes + 2 * state_bytes,
            [
                pltpu.VMEM((3, STORES, tokens, width // STORES), BF16),
                pltpu.SemaphoreType.DMA((3, STORES)),
            ],
            {8 + len(states) + n: n for n in range(len(results))},
        )(places, *inputs, *inner, *states, *results)

    results = outputs(0, (own,), ())
    return tuple(outputs(1, (theirs,), tuple(results)))


def solution(mesh):
    sizes = {"y": 4, "z": 8, "c": 2, "x": 4}
    fine = Mesh(mesh.devices.reshape(tuple(sizes.values())), tuple(sizes))

    def program(queries, key_row_matrix, value_row_matrix, output_gradient):
        scale = float(HEAD * queries.shape[0]) ** -0.5
        spec = P(ROWS, None)
        return jax.shard_map(
            functools.partial(per_device, sizes, scale),
            mesh=fine,
            in_specs=(spec,) * 4,
            out_specs=(spec,) * 3,
            check_vma=False,
        )(queries, key_row_matrix, value_row_matrix, output_gradient)

    return program
```

```python
import functools

import jax
import jax.numpy as jnp
from jax import lax
from jax.experimental import pallas as pl
from jax.experimental.pallas import tpu as pltpu
from jax.sharding import Mesh
from jax.sharding import PartitionSpec as P

HEAD = 128
LOADS = 1
STORES = 4
ROWS = ("x", "y", "z", "c")
SMEM = pl.BlockSpec(memory_space=pltpu.SMEM)
VMEM = pl.BlockSpec(memory_space=pltpu.VMEM)
HBM = pl.BlockSpec(memory_space=pltpu.HBM)
VMEM_LIMIT = 24 * 1024 * 1024
F32, BF16 = jnp.float32, jnp.bfloat16


def contract(lhs, rhs, lhs_dim, rhs_dim):
    return lax.dot_general(
        lhs, rhs, (((lhs_dim,), (rhs_dim,)), ((), ())), preferred_element_type=F32
    )


def load(pairs, sems):
    loads = sems.shape[1]
    width = pairs[0][0].shape[1] // loads
    copies = []
    for n in range(loads):
        lanes = pl.ds(n * width, width)
        for t, (source, target) in enumerate(pairs):
            copy = pltpu.make_async_copy(source.at[:, lanes], target.at[:, lanes], sems.at[t, n])
            copy.start()
            copies.append(copy)
    return copies


def states(pairs, sems, out):
    copies = load(pairs, sems)
    lhs, rhs = (target for _, target in pairs)
    loads = sems.shape[1]
    span = lhs.shape[1] // loads
    for n in range(loads):
        for copy in copies[2 * n : 2 * n + 2]:
            copy.wait()
        for h in range(span // HEAD):
            rows = pl.ds(n * span + h * HEAD, HEAD)
            out[rows, :] = contract(lhs[:, rows], rhs[:, rows], 0, 0)


def send_kernel(core, query, key, value, gradient, send, left, right, sems):
    @pl.when(lax.rem(core[0], 2) == 0)
    def _():
        states(((query, left), (gradient, right)), sems, send)

    @pl.when(lax.rem(core[0], 2) != 0)
    def _():
        states(((value, left), (key, right)), sems, send)


def keep_kernel(core, query, key, value, gradient, keep, q, k, v, g, sems, more):
    @pl.when(lax.rem(core[0], 2) != 0)
    def _():
        rest = load(((key, k), (value, v)), more)
        states(((query, q), (gradient, g)), sems, keep)
        for copy in rest:
            copy.wait()


def inner_products(query, key, value, gradient, gq, gk, gv):
    count = query.shape[0]
    causal = lax.broadcasted_iota(jnp.int32, (count, count), 0) >= lax.broadcasted_iota(
        jnp.int32, (count, count), 1
    )
    for h in range(query.shape[1] // HEAD):
        lanes = pl.ds(h * HEAD, HEAD)
        q, k, v, g = query[:, lanes], key[:, lanes], value[:, lanes], gradient[:, lanes]
        dv = jnp.where(causal, contract(g, v, 1, 1), 0.0).astype(BF16)
        qk = jnp.where(causal, contract(q, k, 1, 1), 0.0).astype(BF16)
        gq[:, lanes] = contract(dv, k, 1, 0)
        gk[:, lanes] = contract(dv, q, 0, 0)
        gv[:, lanes] = contract(qk, g, 0, 0)


def merge_kernel(core, query, key, value, gradient, received, *refs):
    keep, q, k, v, g, chip = refs[5:11]
    inner, sems, more = refs[11:14], refs[14], refs[15]

    @pl.when(lax.rem(core[0], 2) == 0)
    def _():
        rest = load(((query, q), (gradient, g)), more)
        states(((value, v), (key, k)), sems, keep)
        for copy in rest:
            copy.wait()
        inner_products(q, k, v, g, *inner)
        chip[...] = keep[...] + received[...]

    @pl.when(lax.rem(core[0], 2) != 0)
    def _():
        chip[...] = refs[0][...] + received[...]


def onto_kernel(core, own, keep, *refs):
    @pl.when(lax.rem(core[0], 2) != 0)
    def _():
        inner_products(*refs[:4], *refs[8:])

    refs[7][...] = own[...] + keep[...]


def total_kernel(parts, out):
    total = parts[0]
    for n in range(1, parts.shape[0]):
        total = total + parts[n]
    out[...] = total


def scan_kernel(order, places, parts, *refs):
    first = lax.rem(places[0], 2) == 0
    count = parts.shape[0]
    out = refs[-1]
    spot = lax.div(places[0], 2)
    spot = jnp.where(first, spot, len(refs) - 1 - spot)
    total = jnp.zeros(out.shape[1:], F32)
    for step, plane in enumerate(refs[:-1], 1):
        total = total + jnp.where(spot >= step, plane[...], 0.0)
    for n in range(count):
        place = jnp.where(first, order[n], order[count - 1 - n])
        out[place] = total
        total = total + parts[place]


def outputs_kernel(scale, whose, places, query, key, value, gradient, *refs):
    inner = refs[:3]
    sums = refs[3:-5]
    outs = refs[-5:-2]
    held, sems = refs[-2:]
    loads = sems.shape[1]
    part = query.shape[1] // loads

    def state(rows):
        return sums[0][rows, :].astype(BF16)

    def produce(tensors):
        copies = []
        for n in range(loads):
            for h in range(part // HEAD):
                at = n * part + h * HEAD
                lanes = pl.ds(at, HEAD)
                summed = state(lanes)
                for t in tensors:
                    source, dim = ((gradient, 0), (value, 1), (key, 0))[t]
                    result = contract(source[:, lanes], summed, 1, dim)
                    result = result + inner[t][:, lanes]
                    held[t, n, :, pl.ds(h * HEAD, HEAD)] = (scale * result).astype(BF16)
            for t in tensors:
                copy = pltpu.make_async_copy(
                    held.at[t, n], outs[t].at[:, pl.ds(n * part, part)], sems.at[t, n]
                )
                copy.start()
                copies.append(copy)
        for copy in copies:
            copy.wait()

    @pl.when(lax.rem(places[0], 2) == whose)
    def _():
        produce((0,))

    @pl.when(lax.rem(places[0], 2) != whose)
    def _():
        produce((1, 2))


def call(kernel, in_specs, out_specs, out_shape, flops, moved, scratch=(), aliases=None):
    return pl.pallas_call(
        kernel,
        in_specs=in_specs,
        out_specs=out_specs,
        out_shape=out_shape,
        scratch_shapes=scratch,
        input_output_aliases=aliases or {},
        cost_estimate=pl.CostEstimate(flops=flops, bytes_accessed=moved, transcendentals=0),
        compiler_params=pltpu.CompilerParams(vmem_limit_bytes=VMEM_LIMIT),
    )


def order_of(sizes):
    rows, depths = sizes["y"], sizes["z"]
    last = rows * depths - 1
    return [17 * (last - (n % depths * rows + n // depths)) % (last + 1) for n in range(last + 1)]


def exchange(sizes, array):
    order = order_of(sizes)
    members = sorted(range(len(order)), key=lambda n: order[n])
    groups = [
        [(n * sizes["c"] + c) * sizes["x"] + x for n in members]
        for c in range(sizes["c"])
        for x in range(sizes["x"])
    ]
    return lax.all_to_all(
        array, tuple(sizes), 0, 0, tiled=True, axis_index_groups=groups
    )


def onward(array, axis, count, step):
    pairs = [(i, (i + step) % count) for i in range(count)]
    pairs += [(count + i, count + (i - step) % count) for i in range(count)]
    return lax.ppermute(array, ("c", axis), pairs)


def per_device(sizes, scale, queries, key_row_matrix, value_row_matrix, output_gradient):
    tokens, width = queries.shape
    members = sizes["y"] * sizes["z"]
    places = lax.axis_index("c") + 2 * lax.axis_index("x")
    places = places.astype(jnp.int32).reshape(1)
    swap = [(0, 1), (1, 0)]
    product = 2 * width * tokens * HEAD
    token_bytes = 2 * tokens * width
    state_bytes = 4 * width * HEAD
    token_shape = jax.ShapeDtypeStruct((tokens, width), BF16)
    state_shape = jax.ShapeDtypeStruct((width, HEAD), F32)
    parts_shape = jax.ShapeDtypeStruct((members, width // members, HEAD), F32)
    inputs = (queries, key_row_matrix, value_row_matrix, output_gradient)

    inner_shape = jax.ShapeDtypeStruct((tokens, width), F32)
    resting = [pltpu.with_memory_space_constraint(a, pltpu.HBM) for a in inputs]
    send = call(
        send_kernel,
        [SMEM] + [HBM] * 4,
        VMEM,
        state_shape,
        product,
        2 * token_bytes + state_bytes,
        [pltpu.VMEM((tokens, width), BF16)] * 2 + [pltpu.SemaphoreType.DMA((2, LOADS))],
    )(places, *resting)
    received = lax.ppermute(send, "c", swap)
    keep, *inputs = call(
        keep_kernel,
        [SMEM] + [HBM] * 4,
        [VMEM] * 5,
        [state_shape] + [token_shape] * 4,
        product,
        8 * token_bytes + state_bytes,
        [pltpu.SemaphoreType.DMA((2, LOADS))] * 2,
    )(places, *resting)
    received, keep = lax.optimization_barrier((received, keep))
    keep, *rest = call(
        merge_kernel,
        [SMEM] + [HBM] * 4 + [VMEM] * 6,
        [VMEM] * 9,
        [state_shape] + [token_shape] * 4 + [state_shape] + [inner_shape] * 3,
        6 * product,
        14 * token_bytes + 3 * state_bytes,
        [pltpu.SemaphoreType.DMA((2, LOADS))] * 2,
        {6 + n: n for n in range(5)},
    )(places, *resting, received, keep, *inputs)
    inputs, chip, inner = rest[:4], rest[4], rest[5:]
    parts = exchange(sizes, chip.reshape(parts_shape.shape))
    plane = call(
        total_kernel,
        [VMEM],
        VMEM,
        jax.ShapeDtypeStruct(parts_shape.shape[1:], F32),
        width * HEAD,
        state_bytes,
    )(parts)
    planes = [onward(plane, "x", sizes["x"], k) for k in range(1, sizes["x"])]
    prefixes = call(
        functools.partial(scan_kernel, order_of(sizes)),
        [SMEM] + [VMEM] * (1 + len(planes)),
        VMEM,
        parts_shape,
        width * HEAD,
        2 * state_bytes,
    )(places, parts, *planes)
    own = exchange(sizes, prefixes).reshape(width, HEAD)
    onto, *inner = call(
        onto_kernel,
        [SMEM] + [VMEM] * 9,
        [VMEM] * 4,
        [state_shape] + [inner_shape] * 3,
        5 * product,
        10 * token_bytes + 3 * state_bytes,
        aliases={7 + n: 1 + n for n in range(3)},
    )(places, own, keep, *inputs, *inner)
    theirs = lax.ppermute(onto, "c", swap)

    def outputs(whose, states, results):
        return call(
            functools.partial(outputs_kernel, scale, whose),
            [SMEM] + [VMEM] * (7 + len(states)) + [HBM] * len(results),
            [HBM] * 3,
            [token_shape] * 3,
            3 * product // 2,
            7 * token_bytes + 2 * state_bytes,
            [
                pltpu.VMEM((3, STORES, tokens, width // STORES), BF16),
                pltpu.SemaphoreType.DMA((3, STORES)),
            ],
            {8 + len(states) + n: n for n in range(len(results))},
        )(places, *inputs, *inner, *states, *results)

    results = outputs(0, (own,), ())
    return tuple(outputs(1, (theirs,), tuple(results)))


def solution(mesh):
    sizes = {"y": 4, "z": 8, "c": 2, "x": 4}
    fine = Mesh(mesh.devices.reshape(tuple(sizes.values())), tuple(sizes))

    def program(queries, key_row_matrix, value_row_matrix, output_gradient):
        scale = float(HEAD * queries.shape[0]) ** -0.5
        spec = P(ROWS, None)
        return jax.shard_map(
            functools.partial(per_device, sizes, scale),
            mesh=fine,
            in_specs=(spec,) * 4,
            out_specs=(spec,) * 3,
            check_vma=False,
        )(queries, key_row_matrix, value_row_matrix, output_gradient)

    return program
```
